256 devices in a mesh: seq: 32 (over x, y, core), head: 8 (over z).
Axes of the slice: x: 4, y: 4, z: 8, core: 2. Of those that a mesh axis runs over, the one named last changes fastest.
Arguments:
- hidden_in: bfloat16 [16384, 2048], P('seq', 'head'), may hold values from -8 to 8
- proj_weight: bfloat16 [2048, 10240], P(None, 'head'), may hold values from -0.125 to 0.125
- beta_weight: bfloat16 [2048, 32], P(None, 'head'), may hold values from -1 to 1
- norm_gain: float32 [2048], P('head'), may hold values from 0.1 to 1.9
- out_weight: bfloat16 [2048, 2048], P('head'), may hold values from -0.125 to 0.125
- cotangent: bfloat16 [16384, 2048], P('seq', 'head'), may hold values from -6 to 6
Outputs:
- mixed_out: bfloat16 [16384, 2048], P('seq', 'head')
- grad_input: bfloat16 [16384, 2048], P('seq', 'head')
The draws below stay inside these ranges and needn't reach their ends.
All inputs are finite; a program needn't handle non-finite values.
Results may differ from the reference program's by a relative error of at most 0.02.
Values may be sent and summed in bfloat16 or wider, within the bound.
A program may use at most 128 MiB of HBM per device.

```python
import math
import jax
import jax.numpy as jnp
from jax import lax

D = 2048
H = 16
DK = 128
REFL = 2
TOKENS = 16384


def shared_direction(key):
    signs = jax.random.bernoulli(jax.random.fold_in(key, 7001), 0.5, (D,))
    return jnp.where(signs, 1.0, -1.0).astype(jnp.float32) * (6.0 / math.sqrt(D))


def draw_hidden_in(key, part):
    direction = shared_direction(key)
    span = 3 * DK // 4
    starts = jax.random.randint(jax.random.fold_in(key, 7002), (3,), 0, TOKENS - span + 1)
    positions = jnp.arange(TOKENS)
    inside = jnp.any((positions[:, None] >= starts[None, :]) & (positions[:, None] < starts[None, :] + span), axis=1)
    level = jnp.where(inside, 0.0, 1.0).astype(jnp.float32)
    noise_key = jax.random.fold_in(key, 7003)
    noise = jax.random.truncated_normal(noise_key, -6.0, 6.0, (TOKENS, D), jnp.float32)
    return (noise + level[:, None] * direction[None, :]).astype(jnp.bfloat16)


def draw_beta_weight(key, part):
    direction = shared_direction(key)
    pick = jax.random.uniform(jax.random.fold_in(key, 7005), (H,), jnp.float32)
    level = jax.random.uniform(jax.random.fold_in(key, 7006), (H,), jnp.float32)
    align = jnp.where(pick < 0.4, 0.0, 0.55 + 0.55 * level)
    column_align = jnp.repeat(align, REFL)
    base = jax.random.truncated_normal(jax.random.fold_in(key, 7007), -6.0, 6.0, (D, H * REFL), jnp.float32) / math.sqrt(D)
    return (base + 0.25 * direction[:, None] * column_align[None, :]).astype(jnp.bfloat16)


def block_scale(key, shape, cuts, low, high):
    gain, own = 1.0, jax.random.fold_in(key, 6)
    for axis_at, blocks in cuts:
        steps = jnp.exp(jax.random.uniform(jax.random.fold_in(own, axis_at), (blocks,), jnp.float32, low / len(cuts), high / len(cuts)))
        gain = gain * jnp.repeat(steps, shape[axis_at] // blocks).reshape([-1 if axis == axis_at else 1 for axis in range(len(shape))])
    return gain


def bell_draw(own_key, shape, scale, reach, cuts=(), kind=jnp.bfloat16):
    array = jax.random.normal(own_key, shape, jnp.float32) * scale
    if len(cuts) > 0:
        array = block_scale(own_key, shape, cuts, -0.22, 0.18) * array
    return jnp.clip(array, min=-reach, max=reach).astype(kind)


def setup_inputs(seed: int = 0) -> dict:
    key_of = jax.random.split(jax.random.key(seed), 7)
    return {
        "hidden_in": draw_hidden_in(jax.random.fold_in(key_of[6], 71), 0),
        "proj_weight": bell_draw(key_of[1], (D, H * (1 + 2 * REFL) * DK), D ** -0.5, 0.125, ((1, 8),)),
        "beta_weight": draw_beta_weight(jax.random.fold_in(key_of[6], 71), 0),
        "norm_gain": jnp.clip(1.0 + 0.18 * jax.random.normal(key_of[3], (H * DK,), jnp.float32), 0.1, 1.9),
        "out_weight": bell_draw(key_of[4], (H * DK, D), (H * DK) ** -0.5, 0.125, ((0, 8),)),
        "cotangent": bell_draw(key_of[5], (TOKENS, D), 1.0, 6.0, ((0, 32), (1, 8))),
    }


HIGHEST = lax.Precision.HIGHEST

def product(left, right):
    return jnp.matmul(left, right, precision=HIGHEST)

def unit_rows(vectors):
    return vectors / jnp.sqrt(lax.optimization_barrier(jnp.sum(vectors * vectors, axis=-1, keepdims=True)) + 1e-06)

def solve_lower(matrix, target):
    return jax.scipy.linalg.solve_triangular(matrix, target, lower=True, unit_diagonal=True)

def prepare_head(projected, beta_logits, block_size):
    row_count = projected.shape[0]
    key_width = projected.shape[1] // (1 + 2 * REFL)
    blocks = row_count // block_size
    pair_span = block_size * REFL
    pieces = projected.reshape(row_count, 1 + 2 * REFL, key_width)
    queries = unit_rows(pieces[:, 0]).reshape(blocks, block_size, key_width)
    key_rows = unit_rows(pieces[:, 1:1 + REFL]).reshape(blocks, pair_span, key_width)
    values = pieces[:, 1 + REFL:].reshape(blocks, pair_span, key_width)
    strength = (2.0 * jax.nn.sigmoid(beta_logits)).reshape(blocks, pair_span, 1)
    strict_below = jnp.arange(pair_span)[:, None] > jnp.arange(pair_span)[None, :]
    key_gram = strength * product(key_rows, jnp.swapaxes(key_rows, 1, 2))
    lower_unit = jnp.where(strict_below, key_gram, 0.0) + jnp.eye(pair_span, dtype=jnp.float32)
    target = strength * jnp.concatenate([values, key_rows], axis=2)
    solved = jax.vmap(solve_lower)(lower_unit, target)
    return (queries, key_rows, solved[:, :, key_width:], solved[:, :, :key_width])

def read_head(queries, key_rows, shifts, updates, start_state, gain_row):
    block_size = queries.shape[1]
    pair_span = key_rows.shape[1]
    visible = jnp.arange(pair_span)[None, :] <= REFL * jnp.arange(block_size)[:, None] + REFL - 1

    def advance(memory, block_items):
        query_blk, key_blk, shift_blk, update_blk = block_items
        corrected = update_blk - product(shift_blk, memory)
        scores = jnp.where(visible, product(query_blk, key_blk.T), 0.0)
        output = product(query_blk, memory) + product(scores, corrected)
        return (memory + product(key_blk.T, corrected), output)
    _, outputs = lax.scan(advance, start_state, (queries, key_rows, shifts, updates))
    outputs = outputs.reshape(-1, outputs.shape[2])
    inverse_rms = lax.rsqrt(lax.optimization_barrier(jnp.mean(outputs * outputs, axis=-1, keepdims=True)) + 1e-05)
    return outputs * inverse_rms * gain_row

def reference(hidden_in, proj_weight, beta_weight, norm_gain, out_weight, cotangent):
    token_count = hidden_in.shape[0]
    block_size = min(64, token_count)
    head_width = (1 + 2 * REFL) * DK
    proj_heads = jnp.moveaxis(proj_weight.reshape(D, H, head_width), 1, 0)
    beta_heads = jnp.moveaxis(beta_weight.reshape(D, H, REFL), 1, 0)
    out_heads = out_weight.reshape(H, DK, D)
    gain_heads = norm_gain.reshape(H, DK)
    zero_state = jnp.zeros((DK, DK), jnp.float32)
    contract = (((1,), (1,)), ((), ()))

    def one_head(totals, head_items):
        mixed_sum, grad_sum = totals
        proj_head, beta_head, gain_head, out_head = head_items
        projected = jnp.dot(hidden_in.astype(jnp.float32), proj_head.astype(jnp.float32), preferred_element_type=jnp.float32)
        beta_logits = jnp.dot(hidden_in.astype(jnp.float32), beta_head.astype(jnp.float32), preferred_element_type=jnp.float32)

        def forward(proj_now, logit_now):
            prepared = prepare_head(proj_now, logit_now, block_size)
            return read_head(prepared[0], prepared[1], prepared[2], prepared[3], zero_state, gain_head)
        normed, pullback = jax.vjp(forward, projected, beta_logits)
        mixed_sum = mixed_sum + jnp.dot(normed.astype(jnp.bfloat16).astype(jnp.float32), out_head.astype(jnp.float32), preferred_element_type=jnp.float32)
        dnormed = lax.dot_general(cotangent.astype(jnp.float32), out_head.astype(jnp.float32), contract, preferred_element_type=jnp.float32)
        grad_proj, grad_logit = pullback(dnormed)
        grad_sum = grad_sum + lax.dot_general(grad_proj.astype(jnp.bfloat16).astype(jnp.float32), proj_head.astype(jnp.float32), contract, preferred_element_type=jnp.float32)
        grad_sum = grad_sum + lax.dot_general(grad_logit.astype(jnp.bfloat16).astype(jnp.float32), beta_head.astype(jnp.float32), contract, preferred_element_type=jnp.float32)
        return ((mixed_sum, grad_sum), None)
    zeros_out = jnp.zeros((token_count, D), jnp.float32)
    (mixed_sum, grad_sum), _ = lax.scan(one_head, (zeros_out, zeros_out), (proj_heads, beta_heads, gain_heads, out_heads))
    return (mixed_sum.astype(jnp.bfloat16), grad_sum.astype(jnp.bfloat16))
```

```python
import jax
import jax.numpy as jnp
from jax import lax
from jax.experimental import pallas as pl
from jax.experimental.pallas import tpu as pltpu
from jax.sharding import PartitionSpec as P

DK = 128
REFL = 2
CT = 64
CR = CT * REFL
MESH = pl.DeviceIdType.MESH
F32 = jnp.float32
BF16 = jnp.bfloat16
VM = pl.BlockSpec(memory_space=pltpu.VMEM)


def split(a):
    hi = a.astype(BF16)
    lo = (a - hi.astype(F32)).astype(BF16)
    return hi, lo


def lhs(a):
    hi, lo = split(a)
    return jnp.concatenate([hi, lo], axis=1)


def rhs(b):
    hi, lo = split(b)
    row = jnp.concatenate([hi, lo], axis=1)
    return jnp.concatenate([row, row], axis=0)


def pmm(a2, b4):
    n = b4.shape[1] // 2
    r = jnp.dot(a2, b4, preferred_element_type=F32)
    return r[:, :n] + r[:, n:]


def mm(a, b):
    return pmm(lhs(a), rhs(b))


def mmt(a, b):
    return pmm(lhs(a.T), rhs(b))


def orders(rows, cols, row_tokens, col_tokens):
    r = lax.broadcasted_iota(jnp.int32, (rows, cols), 0)
    c = lax.broadcasted_iota(jnp.int32, (rows, cols), 1)
    if row_tokens:
        r_at = r
    else:
        r_at = 2 * (r % CT) + r // CT
    c_at = 2 * (c % CT) + c // CT
    return r_at, c_at


def unit_scale(v, eps):
    return lax.rsqrt(jnp.sum(v * v, axis=1, keepdims=True) + eps)


def head_rows(proj_ref, c, h):
    rows = pl.ds(pl.multiple_of(c * CT, CT), CT)
    base = h * 5 * DK
    return [proj_ref[rows, base + i * DK : base + (i + 1) * DK] for i in range(5)]


def strengths(logit_ref, c, h):
    rows = pl.ds(pl.multiple_of(c * CT, CT), CT)
    x = jnp.concatenate(
        [logit_ref[rows, 2 * h : 2 * h + 1], logit_ref[rows, 2 * h + 1 : 2 * h + 2]], axis=0
    )
    return 1.0 / (1.0 + jnp.exp(-x)), 1.0 / (1.0 + jnp.exp(x))


def crows(c):
    return pl.ds(pl.multiple_of(c * CR, CR), CR)


def trows(c):
    return pl.ds(pl.multiple_of(c * CT, CT), CT)


def place():
    s = lax.axis_index("seq")
    core = lax.rem(s, 2)
    y = lax.rem(lax.div(s, 2), 4)
    x = lax.div(s, 8)
    return x, y, core


def at(x, y, core):
    return (x * 4 + y) * 2 + core


def meet(x, y, core):
    barrier = pltpu.get_barrier_semaphore()
    peers = [at(x, y, 1 - core)]
    for d in (1, 2, 3):
        peers.append(at(x, lax.rem(y + d, 4), core))
        peers.append(at(lax.rem(x + d, 4), y, core))
    for p in peers:
        pl.semaphore_signal(barrier, inc=1, device_id={"seq": p}, device_id_type=MESH)
    pl.semaphore_wait(barrier, len(peers))


def send(src, dst, sems, i, seq):
    return pltpu.make_async_remote_copy(
        src_ref=src,
        dst_ref=dst,
        send_sem=sems.at[0, i],
        recv_sem=sems.at[1, i],
        device_id={"seq": seq},
        device_id_type=MESH,
    )


def compose(later, earlier):
    r = mm(later[:, :DK], earlier)
    return jnp.concatenate([r[:, :DK], r[:, DK:] + later[:, DK:]], axis=1)


def prep_kernel(
    proj, logit,
    q_o, k_o, w_o, uv_o, t_o, a_o, pm_o, po_o, mc_o, start_o, msave_o,
    oc, mo, cslot, yslot, xslot, fin, sems,
):
    heads = 2
    chunks = proj.shape[0] // CT
    x, y, core = place()
    meet(x, y, core)

    def chunk_pair(step, carry):
        r_at, c_at = orders(CR, CR, False, False)
        below = r_at > c_at
        diff = jnp.bitwise_xor(r_at, c_at)
        tr, tc = orders(CT, CR, True, False)
        visible = tc <= 2 * tr + 1
        eye = jnp.where(r_at == c_at, 1.0, 0.0)
        jobs = [(h, 2 * step + cc) for cc in range(2) for h in range(heads)]
        ks, bs, vs, qs = [], [], [], []
        for h, c in jobs:
            a, c1, c2, v1, v2 = head_rows(proj, c, h)
            q = a * unit_scale(a, 1e-6)
            k = jnp.concatenate([c1 * unit_scale(c1, 1e-6), c2 * unit_scale(c2, 1e-6)], axis=0)
            sig, _ = strengths(logit, c, h)
            ks.append(k)
            qs.append(q)
            bs.append(2.0 * sig)
            vs.append(jnp.concatenate([v1, v2], axis=0))
            q_o[h, trows(c), :] = q
            k_o[h, crows(c), :] = k
        kts = [k.T for k in ks]
        kt4 = [rhs(kt) for kt in kts]
        grams = [pmm(lhs(jnp.concatenate([k, q], axis=0)), b4) for k, q, b4 in zip(ks, qs, kt4)]
        for (h, c), g in zip(jobs, grams):
            a_o[h, trows(c), :] = jnp.where(visible, g[CR:], 0.0)
        ns = [jnp.where(below, b * g[:CR], 0.0) for b, g in zip(bs, grams)]
        ts = [eye - jnp.where(diff == 1, n, 0.0) for n in ns]
        level = 1
        while (1 << level) < CR:
            parts = [jnp.where((diff >> level) == 1, n, 0.0) for n in ns]
            inner = [mm(p, t) for p, t in zip(parts, ts)]
            outer = [mm(t, i) for t, i in zip(ts, inner)]
            ts = [t - o for t, o in zip(ts, outer)]
            level += 1
        wus = [mm(t, b * jnp.concatenate([k, v], axis=1)) for t, b, k, v in zip(ts, bs, ks, vs)]
        mos = [pmm(lhs(kt), rhs(wu)) for kt, wu in zip(kts, wus)]
        for (h, c), t, wu, m in zip(jobs, ts, wus, mos):
            t_o[h, crows(c), :] = t
            w_o[h, crows(c), :] = wu[:, :DK]
            uv_o[h, crows(c), :] = wu[:, DK:]
            mc_o[h, crows(c), :] = eye_nat() - m[:, :DK]
            oc[h, crows(c), :] = m[:, DK:]
        return carry

    lax.fori_loop(0, chunks // 2, chunk_pair, 0)

    for h in range(heads):
        mo[h, :, :DK] = eye_nat()
        mo[h, :, DK:] = jnp.zeros((DK, DK), F32)

    def prefix(c, carry):
        for h in range(heads):
            cur = mo[h]
            pm_o[h, crows(c), :] = cur[:, :DK]
            po_o[h, crows(c), :] = cur[:, DK:]
            r = mm(mc_o[h, crows(c), :], cur)
            mo[h, :, :DK] = r[:, :DK]
            mo[h, :, DK:] = r[:, DK:] + oc[h, crows(c), :]
        return carry

    lax.fori_loop(0, chunks, prefix, 0)

    c0 = send(mo.at[1 - core], cslot.at[core], sems, 0, at(x, y, 1 - core))
    c0.start()
    cslot[core] = mo[core]
    c0.wait()
    first = cslot[0]
    chip = compose(cslot[1], first)
    yslot[0] = chip
    sends = [
        send(yslot.at[0], yslot.at[d], sems, d, at(x, lax.rem(y + d, 4), core)) for d in (1, 2, 3)
    ]
    for c in sends:
        c.start()
    for c in sends:
        c.wait()
    got = [yslot[lax.rem(y + 4 - i, 4)] for i in range(4)]
    p1 = got[0]
    p2 = compose(got[1], p1)
    p3 = compose(got[2], p2)
    total = compose(got[3], p3)
    xslot[0] = total
    sends = [
        send(xslot.at[0], xslot.at[d], sems, 3 + d, at(lax.rem(x + d, 4), y, core))
        for d in (1, 2, 3)
    ]
    for c in sends:
        c.start()
    before = jnp.where(y == 1, p1, jnp.where(y == 2, p2, p3))
    for i in range(2):
        msave_o[i] = cslot[i, :, :DK]
    for i in range(4):
        msave_o[2 + i] = got[i][:, :DK]
    for c in sends:
        c.wait()
    gx = [xslot[lax.rem(x + 4 - i, 4)] for i in range(4)]
    for i in range(4):
        msave_o[6 + i] = gx[i][:, :DK]
    s1 = gx[0][:, DK:]
    s2 = mm(gx[1][:, :DK], s1) + gx[1][:, DK:]
    s3 = mm(gx[2][:, :DK], s2) + gx[2][:, DK:]
    group = jnp.where(x == 0, 0.0, jnp.where(x == 1, s1, jnp.where(x == 2, s2, s3)))
    s_chip = jnp.where(y == 0, group, mm(before[:, :DK], group) + before[:, DK:])
    s_next = mm(first[:, :DK], s_chip) + first[:, DK:]
    fin[2] = jnp.where(core == 0, s_next, s_chip)
    c1 = send(fin.at[2], fin.at[core], sems, 7, at(x, y, 1 - core))
    c1.start()
    fin[core] = jnp.where(core == 0, s_chip, s_next)
    c1.wait()
    start_o[0] = fin[0]
    start_o[1] = fin[1]


def eye_nat():
    r = lax.broadcasted_iota(jnp.int32, (DK, DK), 0)
    c = lax.broadcasted_iota(jnp.int32, (DK, DK), 1)
    return jnp.where(r == c, 1.0, 0.0)


def read_kernel(
    proj, logit, gain, dn, q_i, k_i, w_i, uv_i, t_i, a_i, pm_i, po_i, mc_i, start_i, msave_i,
    normed_o, gproj_o, glogit_o,
    s_s, u_s, do_s, y_s, e_s, d_s, esum, ec, yslot, xslot, fin, sems,
):
    heads = 2
    chunks = proj.shape[0] // CT
    x, y, core = place()
    meet(x, y, core)
    for h in range(heads):
        esum[h] = jnp.zeros((DK, DK), F32)

    def forward(step, carry):
        jobs = [(h, 2 * step + cc) for cc in range(2) for h in range(heads)]
        starts = [rhs(start_i[h]) for h in range(heads)]
        states = [
            pmm(lhs(pm_i[h, crows(c), :]), starts[h]) + po_i[h, crows(c), :] for h, c in jobs
        ]
        s4 = [rhs(s) for s in states]
        wq = [
            pmm(lhs(jnp.concatenate([w_i[h, crows(c), :], q_i[h, trows(c), :]], axis=0)), b)
            for (h, c), b in zip(jobs, s4)
        ]
        us = [uv_i[h, crows(c), :] - r[:CR] for (h, c), r in zip(jobs, wq)]
        outs = [r[CR:] + mm(a_i[h, trows(c), :], u) for (h, c), r, u in zip(jobs, wq, us)]
        dos = []
        for (h, c), s, u, o in zip(jobs, states, us, outs):
            g = gain[h : h + 1, :]
            r = lax.rsqrt(jnp.mean(o * o, axis=1, keepdims=True) + 1e-5)
            normed_o[trows(c), h * DK : (h + 1) * DK] = (o * r * g).astype(BF16)
            dy = dn[trows(c), h * DK : (h + 1) * DK] * g
            back = jnp.mean(o * dy, axis=1, keepdims=True)
            do = r * (dy - o * (r * r * back))
            dos.append(do)
            s_s[h, crows(c), :] = s
            u_s[h, crows(c), :] = u
            do_s[h, trows(c), :] = do
        ys = [mmt(a_i[h, trows(c), :], do) for (h, c), do in zip(jobs, dos)]
        es = [
            mmt(q_i[h, trows(c), :], do) - mmt(w_i[h, crows(c), :], yy)
            for (h, c), do, yy in zip(jobs, dos, ys)
        ]
        adds = [mmt(pm_i[h, crows(c), :], e) for (h, c), e in zip(jobs, es)]
        for (h, c), yy, e, add in zip(jobs, ys, es, adds):
            y_s[h, crows(c), :] = yy
            e_s[h, crows(c), :] = e
            esum[h] += add
        return carry

    lax.fori_loop(0, chunks // 2, forward, 0)

    c0 = send(esum.at[1 - core], ec.at[core], sems, 0, at(x, y, 1 - core))
    c0.start()
    ec[core] = esum[core]
    c0.wait()
    e1 = ec[1]
    yslot[0] = mmt(msave_i[0], e1) + ec[0]
    sends = [
        send(yslot.at[0], yslot.at[d], sems, d, at(x, lax.rem(y + d, 4), core)) for d in (1, 2, 3)
    ]
    for c in sends:
        c.start()
    my = [msave_i[2 + i] for i in range(4)]
    suf1 = mm(my[3], my[2])
    suf0 = mm(suf1, my[1])
    suf = jnp.where(y == 2, my[3], jnp.where(y == 1, suf1, suf0))
    for c in sends:
        c.wait()
    got = [yslot[lax.rem(y + 4 - i, 4)] for i in range(4)]
    r3 = got[3]
    r2 = mmt(my[2], r3) + got[2]
    r1 = mmt(my[1], r2) + got[1]
    xslot[0] = mmt(my[0], r1) + got[0]
    sends = [
        send(xslot.at[0], xslot.at[d], sems, 3 + d, at(lax.rem(x + d, 4), y, core))
        for d in (1, 2, 3)
    ]
    for c in sends:
        c.start()
    inside = jnp.where(y == 2, r3, jnp.where(y == 1, r2, r1))
    for c in sends:
        c.wait()
    gx = [xslot[lax.rem(x + 4 - i, 4)] for i in range(4)]
    x2 = gx[3]
    x1 = mmt(msave_i[8], x2) + gx[2]
    x0 = mmt(msave_i[7], x1) + gx[1]
    group = jnp.where(x == 3, 0.0, jnp.where(x == 2, x2, jnp.where(x == 1, x1, x0)))
    d_chip = jnp.where(y == 3, group, mmt(suf, group) + inside)
    d_prev = mmt(msave_i[1], d_chip) + e1
    fin[2] = jnp.where(core == 1, d_prev, d_chip)
    c1 = send(fin.at[2], fin.at[core], sems, 7, at(x, y, 1 - core))
    c1.start()
    fin[core] = jnp.where(core == 1, d_chip, d_prev)
    c1.wait()

    def chain(step, carry):
        c = chunks - 1 - step
        for h in range(heads):
            cur = fin[h]
            d_s[h, crows(c), :] = cur
            fin[h] = mmt(mc_i[h, crows(c), :], cur) + e_s[h, crows(c), :]
        return carry

    lax.fori_loop(0, chunks, chain, 0)

    def backward(step, carry):
        r_at, c_at = orders(CR, CR, False, False)
        below = r_at > c_at
        tr, tc = orders(CT, CR, True, False)
        visible = tc <= 2 * tr + 1
        jobs = [(h, 2 * step + cc) for cc in range(2) for h in range(heads)]
        ks = [k_i[h, crows(c), :] for h, c in jobs]
        k4 = [rhs(k) for k in ks]
        ds = [d_s[h, crows(c), :] for h, c in jobs]
        us = [u_s[h, crows(c), :] for h, c in jobs]
        dus = [mm(k, d) + y_s[h, crows(c), :] for (h, c), k, d in zip(jobs, ks, ds)]
        zs = [mmt(t_i[h, crows(c), :], du) for (h, c), du in zip(jobs, dus)]
        sigs = [strengths(logit, c, h) for h, c in jobs]
        bzs = [2.0 * sg[0] * z for sg, z in zip(sigs, zs)]
        dos = [do_s[h, trows(c), :] for h, c in jobs]
        both = [lhs(jnp.concatenate([bz, do], axis=0)) for bz, do in zip(bzs, dos)]
        pus = [pmm(b2, rhs(u.T)) for b2, u in zip(both, us)]
        pss = [pmm(b2, rhs(s_s[h, crows(c), :].T)) for (h, c), b2 in zip(jobs, both)]
        pbs = [jnp.where(below, p[:CR], 0.0) for p in pus]
        das = [jnp.where(visible, p[CR:], 0.0) for p in pus]
        mixes = [
            pmm(lhs(jnp.concatenate([pb + pb.T, da], axis=0)), kk)
            for pb, da, kk in zip(pbs, das, k4)
        ]
        dks = [
            mm(u, d.T) - ps[:CR] - mx[:CR] + mmt(da, q_i[h, trows(c), :])
            for (h, c), u, d, ps, mx, da in zip(jobs, us, ds, pss, mixes, das)
        ]
        dqs = [mx[CR:] + ps[CR:] for mx, ps in zip(mixes, pss)]
        for (h, c), k, u, z, bz, sg, dk, dq in zip(jobs, ks, us, zs, bzs, sigs, dks, dqs):
            a, c1, c2, _, _ = head_rows(proj, c, h)
            q = q_i[h, trows(c), :]
            sa = unit_scale(a, 1e-6)
            sc = jnp.concatenate([unit_scale(c1, 1e-6), unit_scale(c2, 1e-6)], axis=0)
            ga = sa * (dq - q * jnp.sum(q * dq, axis=1, keepdims=True))
            gc = sc * (dk - k * jnp.sum(k * dk, axis=1, keepdims=True))
            base = h * 5 * DK
            gproj_o[trows(c), base : base + DK] = ga.astype(BF16)
            gproj_o[trows(c), base + DK : base + 2 * DK] = gc[:CT].astype(BF16)
            gproj_o[trows(c), base + 2 * DK : base + 3 * DK] = gc[CT:].astype(BF16)
            gproj_o[trows(c), base + 3 * DK : base + 4 * DK] = bz[:CT].astype(BF16)
            gproj_o[trows(c), base + 4 * DK : base + 5 * DK] = bz[CT:].astype(BF16)
            gl = jnp.sum(z * u, axis=1, keepdims=True) * sg[1]
            glogit_o[trows(c), 2 * h : 2 * h + 1] = gl[:CT].astype(BF16)
            glogit_o[trows(c), 2 * h + 1 : 2 * h + 2] = gl[CT:].astype(BF16)
        return carry

    lax.fori_loop(0, chunks // 2, backward, 0)


def params(collective_id, mib):
    return pltpu.CompilerParams(
        collective_id=collective_id, has_side_effects=True, vmem_limit_bytes=mib << 20
    )


def prepare(projected, logits):
    rows = projected.shape[0]
    h2 = lambda r: jax.ShapeDtypeStruct((2, r, DK), F32)
    full = h2(REFL * rows)
    return pl.pallas_call(
        prep_kernel,
        out_shape=[
            h2(rows), full, full, full, full, h2(rows), full, full, full, h2(DK),
            jax.ShapeDtypeStruct((10, DK, DK), F32),
        ],
        in_specs=[VM, VM],
        out_specs=[VM] * 11,
        scratch_shapes=[
            pltpu.VMEM((2, REFL * rows, DK), F32),
            pltpu.VMEM((2, DK, 2 * DK), F32),
            pltpu.VMEM((2, DK, 2 * DK), F32),
            pltpu.VMEM((4, DK, 2 * DK), F32),
            pltpu.VMEM((4, DK, 2 * DK), F32),
            pltpu.VMEM((3, DK, DK), F32),
            pltpu.SemaphoreType.DMA((2, 8)),
        ],
        compiler_params=params(1, 48),
    )(projected, logits)


def read_back(projected, logits, gains, dnormed, prepared):
    rows = projected.shape[0]
    full = pltpu.VMEM((2, REFL * rows, DK), F32)
    part = pltpu.VMEM((2, rows, DK), F32)
    return pl.pallas_call(
        read_kernel,
        out_shape=[
            jax.ShapeDtypeStruct((rows, 2 * DK), BF16),
            jax.ShapeDtypeStruct((rows, 10 * DK), BF16),
            jax.ShapeDtypeStruct((rows, 4), BF16),
        ],
        in_specs=[VM] * (4 + len(prepared)),
        out_specs=[VM] * 3,
        scratch_shapes=[
            full, full, part, full, full, full,
            pltpu.VMEM((2, DK, DK), F32),
            pltpu.VMEM((2, DK, DK), F32),
            pltpu.VMEM((4, DK, DK), F32),
            pltpu.VMEM((4, DK, DK), F32),
            pltpu.VMEM((3, DK, DK), F32),
            pltpu.SemaphoreType.DMA((2, 8)),
        ],
        compiler_params=params(2, 56),
    )(projected, logits, gains, dnormed, *prepared)


def local(hidden_in, proj_weight, beta_weight, norm_gain, out_weight, cotangent):
    contract = (((1,), (1,)), ((), ()))
    hidden_part = lax.all_gather(hidden_in, "head", axis=1, tiled=True)
    projected = jnp.dot(hidden_part, proj_weight, preferred_element_type=F32)
    logits = jnp.dot(hidden_part, beta_weight, preferred_element_type=F32)
    cotangent, projected = lax.optimization_barrier((cotangent, projected))
    cot_part = lax.all_gather(cotangent, "head", axis=1, tiled=True)
    prepared = prepare(projected, logits)
    dnormed = lax.dot_general(cot_part, out_weight, contract, preferred_element_type=F32)
    normed, grad_proj, grad_logit = read_back(
        projected, logits, norm_gain.reshape(2, DK), dnormed, prepared
    )
    mixed_terms = jnp.dot(normed, out_weight, preferred_element_type=F32)
    mixed_out = lax.psum_scatter(
        mixed_terms.astype(BF16), "head", scatter_dimension=1, tiled=True
    )
    input_term = lax.dot_general(grad_proj, proj_weight, contract, preferred_element_type=F32)
    input_term = input_term + lax.dot_general(
        grad_logit, beta_weight, contract, preferred_element_type=F32
    )
    grad_input = lax.psum_scatter(
        input_term.astype(BF16), "head", scatter_dimension=1, tiled=True
    )
    return (mixed_out, grad_input)


def solution(mesh):
    placed = (
        P("seq", "head"),
        P(None, "head"),
        P(None, "head"),
        P("head"),
        P("head", None),
        P("seq", "head"),
    )
    return jax.shard_map(
        local,
        mesh=mesh,
        in_specs=placed,
        out_specs=(P("seq", "head"), P("seq", "head")),
        check_vma=False,
    )
```

```python
import jax
import jax.numpy as jnp
from jax import lax
from jax.experimental import pallas as pl
from jax.experimental.pallas import tpu as pltpu
from jax.sharding import PartitionSpec as P

DK = 128
REFL = 2
CT = 64
CR = CT * REFL
MESH = pl.DeviceIdType.MESH
F32 = jnp.float32
BF16 = jnp.bfloat16
VM = pl.BlockSpec(memory_space=pltpu.VMEM)


def split(a):
    hi = a.astype(BF16)
    lo = (a - hi.astype(F32)).astype(BF16)
    return hi, lo


def lhs(a):
    hi, lo = split(a)
    return jnp.concatenate([hi, lo], axis=1)


def rhs(b):
    hi, lo = split(b)
    row = jnp.concatenate([hi, lo], axis=1)
    return jnp.concatenate([row, row], axis=0)


def pmm(a2, b4):
    n = b4.shape[1] // 2
    r = jnp.dot(a2, b4, preferred_element_type=F32)
    return r[:, :n] + r[:, n:]


def mm(a, b):
    return pmm(lhs(a), rhs(b))


def mmt(a, b):
    return pmm(lhs(a.T), rhs(b))


def orders(rows, cols, row_tokens, col_tokens):
    r = lax.broadcasted_iota(jnp.int32, (rows, cols), 0)
    c = lax.broadcasted_iota(jnp.int32, (rows, cols), 1)
    if row_tokens:
        r_at = r
    else:
        r_at = 2 * (r % CT) + r // CT
    c_at = 2 * (c % CT) + c // CT
    return r_at, c_at


def unit_scale(v, eps):
    return lax.rsqrt(jnp.sum(v * v, axis=1, keepdims=True) + eps)


def head_rows(proj_ref, c, h):
    rows = pl.ds(pl.multiple_of(c * CT, CT), CT)
    base = h * 5 * DK
    return [proj_ref[rows, base + i * DK : base + (i + 1) * DK] for i in range(5)]


def strengths(logit_ref, c, h):
    rows = pl.ds(pl.multiple_of(c * CT, CT), CT)
    x = jnp.concatenate(
        [logit_ref[rows, 2 * h : 2 * h + 1], logit_ref[rows, 2 * h + 1 : 2 * h + 2]], axis=0
    )
    return 1.0 / (1.0 + jnp.exp(-x)), 1.0 / (1.0 + jnp.exp(x))


def crows(c):
    return pl.ds(pl.multiple_of(c * CR, CR), CR)


def trows(c):
    return pl.ds(pl.multiple_of(c * CT, CT), CT)


def place():
    s = lax.axis_index("seq")
    core = lax.rem(s, 2)
    y = lax.rem(lax.div(s, 2), 4)
    x = lax.div(s, 8)
    return x, y, core


def at(x, y, core):
    return (x * 4 + y) * 2 + core


def meet(x, y, core, z):
    barrier = pltpu.get_barrier_semaphore()
    peers = [{"seq": at(x, y, 1 - core)}]
    for d in (1, 2, 3):
        peers.append({"seq": at(x, lax.rem(y + d, 4), core)})
        peers.append({"seq": at(lax.rem(x + d, 4), y, core)})
    peers.append({"head": lax.rem(z + 1, 8)})
    peers.append({"head": lax.rem(z + 7, 8)})
    for p in peers:
        pl.semaphore_signal(barrier, inc=1, device_id=p, device_id_type=MESH)
    pl.semaphore_wait(barrier, len(peers))


RIGHT, LEFT = 0, 1
HALF = 256


def beside(z, way):
    return {"head": lax.rem(z + (1 if way == RIGHT else 7), 8)}


def gather_unit(buf, sems, z, way, d, j):
    src, dst = (d - 1, d) if way == RIGHT else ((9 - d) % 8, 8 - d)
    rows = pl.ds(j * HALF, HALF)
    return pltpu.make_async_remote_copy(
        src_ref=buf.at[src, rows],
        dst_ref=buf.at[dst, rows],
        send_sem=sems.at[0, way, d - 1, j],
        recv_sem=sems.at[1, way, d - 1, j],
        device_id=beside(z, way),
        device_id_type=MESH,
    )


def gather_has(way, d, j):
    return d < 4 or (d == 4 and j == way)


def gather_start(buf, sems, z):
    for j in (0, 1):
        for way in (RIGHT, LEFT):
            gather_unit(buf, sems, z, way, 1, j).start()


def gather_step(buf, sems, z, d):
    for j in (0, 1):
        for way in (RIGHT, LEFT):
            if gather_has(way, d, j):
                gather_unit(buf, sems, z, way, d, j).wait_recv()
                if gather_has(way, d + 1, j):
                    gather_unit(buf, sems, z, way, d + 1, j).start()


def gather_end(buf, sems, z):
    for d in (1, 2, 3, 4):
        for j in (0, 1):
            for way in (RIGHT, LEFT):
                if gather_has(way, d, j):
                    gather_unit(buf, sems, z, way, d, j).wait_send()


class Scatter:
    def __init__(self, own, out, sent, came, sems, z):
        self.own, self.out, self.sent, self.came, self.sems, self.z = own, out, sent, came, sems, z

    def unit(self, way, s, j):
        rows = pl.ds(j * HALF, HALF)
        return pltpu.make_async_remote_copy(
            src_ref=self.sent.at[way, s, rows],
            dst_ref=self.came.at[way, s, rows],
            send_sem=self.sems.at[0, way, s, j],
            recv_sem=self.sems.at[1, way, s, j],
            device_id=beside(self.z, way),
            device_id_type=MESH,
        )

    def has(self, way, s, j):
        return s > 0 or j == way

    def step(self, way, s, j):
        if not self.has(way, s, j):
            return
        rows = slice(j * HALF, (j + 1) * HALF)
        dest = lax.rem(self.z + ((4 - s) if way == RIGHT else (4 + s)), 8)
        term = self.own(dest, j)
        if s > 0 and self.has(way, s - 1, j):
            self.unit(way, s - 1, j).wait_recv()
            term = term + self.came[way, s - 1, rows].astype(F32)
        self.sent[way, s, rows] = term.astype(BF16)
        self.unit(way, s, j).start()

    def finish(self):
        for j in (0, 1):
            rows = slice(j * HALF, (j + 1) * HALF)
            term = self.own(self.z, j)
            for way in (RIGHT, LEFT):
                self.unit(way, 3, j).wait_recv()
                term = term + self.came[way, 3, rows].astype(F32)
            self.out[rows, :] = term.astype(BF16)
        for way in (RIGHT, LEFT):
            for s in range(4):
                for j in (0, 1):
                    if self.has(way, s, j):
                        self.unit(way, s, j).wait_send()


def send(src, dst, sems, i, seq):
    return pltpu.make_async_remote_copy(
        src_ref=src,
        dst_ref=dst,
        send_sem=sems.at[0, i],
        recv_sem=sems.at[1, i],
        device_id={"seq": seq},
        device_id_type=MESH,
    )


def compose(later, earlier):
    r = mm(later[:, :DK], earlier)
    return jnp.concatenate([r[:, :DK], r[:, DK:] + later[:, DK:]], axis=1)


def eye_nat():
    r = lax.broadcasted_iota(jnp.int32, (DK, DK), 0)
    c = lax.broadcasted_iota(jnp.int32, (DK, DK), 1)
    return jnp.where(r == c, 1.0, 0.0)


CONTRACT = (((1,), (1,)), ((), ()))


def layer_kernel(
    hid, pw, bw, gain, ow, cot,
    mixed_o, grad_o,
    hids, cots, pw_v, ow_v, proj, logit, dn,
    q_i, k_i, w_i, uv_i, t_i, a_i, pm_i, po_i, mc_i, start_i, msave_i,
    oc, mo, cslot, yslot_f, xslot_f, fin_f,
    s_s, u_s, do_s, y_s, e_s, d_s, esum, ec, yslot_b, xslot_b, fin_b,
    normed, gproj, glogit, msent, mcame, gsent, gcame,
    sems_h, sems_c, sems_f, sems_b, sems_m, sems_g, sems_w,
):
    heads = 2
    chunks = proj.shape[0] // CT
    x, y, core = place()
    z = lax.axis_index("head")
    pw_copy = pltpu.make_async_copy(pw, pw_v, sems_w.at[0])
    ow_copy = pltpu.make_async_copy(ow, ow_v, sems_w.at[1])
    pw_copy.start()
    ow_copy.start()
    hids[0] = hid[...]
    cots[0] = cot[...]
    meet(x, y, core, z)

    gather_start(hids, sems_h, z)
    pw_copy.wait()
    for d in range(5):
        if d > 0:
            gather_step(hids, sems_h, z, d)
        if d == 3:
            gather_start(cots, sems_c, z)
        for i in {d, (8 - d) % 8}:
            rows = pl.ds(pl.multiple_of(lax.rem(z + 8 - i, 8) * HALF, HALF), HALF)
            part = jnp.dot(hids[i], pw_v[rows, :], preferred_element_type=F32)
            part_b = jnp.dot(hids[i], bw[rows, :], preferred_element_type=F32)
            proj[...] = part if i == 0 else proj[...] + part
            logit[...] = part_b if i == 0 else logit[...] + part_b

    def chunk_pair(step, carry):
        for d in (1, 2, 3):
            pl.when(step == d)(lambda d=d: gather_step(cots, sems_c, z, d))
        r_at, c_at = orders(CR, CR, False, False)
        below = r_at > c_at
        diff = jnp.bitwise_xor(r_at, c_at)
        tr, tc = orders(CT, CR, True, False)
        visible = tc <= 2 * tr + 1
        eye = jnp.where(r_at == c_at, 1.0, 0.0)
        jobs = [(h, 2 * step + cc) for cc in range(2) for h in range(heads)]
        ks, bs, vs, qs = [], [], [], []
        for h, c in jobs:
            a, c1, c2, v1, v2 = head_rows(proj, c, h)
            q = a * unit_scale(a, 1e-6)
            k = jnp.concatenate([c1 * unit_scale(c1, 1e-6), c2 * unit_scale(c2, 1e-6)], axis=0)
            sig, _ = strengths(logit, c, h)
            ks.append(k)
            qs.append(q)
            bs.append(2.0 * sig)
            vs.append(jnp.concatenate([v1, v2], axis=0))
            q_i[h, trows(c), :] = q
            k_i[h, crows(c), :] = k
        kts = [k.T for k in ks]
        kt4 = [rhs(kt) for kt in kts]
        grams = [pmm(lhs(jnp.concatenate([k, q], axis=0)), b4) for k, q, b4 in zip(ks, qs, kt4)]
        for (h, c), g in zip(jobs, grams):
            a_i[h, trows(c), :] = jnp.where(visible, g[CR:], 0.0)
        ns = [jnp.where(below, b * g[:CR], 0.0) for b, g in zip(bs, grams)]
        ts = [eye - jnp.where(diff == 1, n, 0.0) for n in ns]
        level = 1
        while (1 << level) < CR:
            parts = [jnp.where((diff >> level) == 1, n, 0.0) for n in ns]
            inner = [mm(p, t) for p, t in zip(parts, ts)]
            outer = [mm(t, i) for t, i in zip(ts, inner)]
            ts = [t - o for t, o in zip(ts, outer)]
            level += 1
        wus = [mm(t, b * jnp.concatenate([k, v], axis=1)) for t, b, k, v in zip(ts, bs, ks, vs)]
        mos = [pmm(lhs(kt), rhs(wu)) for kt, wu in zip(kts, wus)]
        for (h, c), t, wu, m in zip(jobs, ts, wus, mos):
            t_i[h, crows(c), :] = t
            w_i[h, crows(c), :] = wu[:, :DK]
            uv_i[h, crows(c), :] = wu[:, DK:]
            mc_i[h, crows(c), :] = eye_nat() - m[:, :DK]
            oc[h, crows(c), :] = m[:, DK:]
        return carry

    lax.fori_loop(0, chunks // 2, chunk_pair, 0)

    gather_step(cots, sems_c, z, 4)

    for h in range(heads):
        mo[h, :, :DK] = eye_nat()
        mo[h, :, DK:] = jnp.zeros((DK, DK), F32)

    def prefix(c, carry):
        for h in range(heads):
            cur = mo[h]
            pm_i[h, crows(c), :] = cur[:, :DK]
            po_i[h, crows(c), :] = cur[:, DK:]
            r = mm(mc_i[h, crows(c), :], cur)
            mo[h, :, :DK] = r[:, :DK]
            mo[h, :, DK:] = r[:, DK:] + oc[h, crows(c), :]
        return carry

    lax.fori_loop(0, chunks, prefix, 0)

    c0 = send(mo.at[1 - core], cslot.at[core], sems_f, 0, at(x, y, 1 - core))
    c0.start()
    cslot[core] = mo[core]
    c0.wait()
    first = cslot[0]
    chip = compose(cslot[1], first)
    yslot_f[0] = chip
    sends = [
        send(yslot_f.at[0], yslot_f.at[d], sems_f, d, at(x, lax.rem(y + d, 4), core)) for d in (1, 2, 3)
    ]
    for c in sends:
        c.start()
    ow_copy.wait()
    for i in range(8):
        cols = pl.ds(pl.multiple_of(lax.rem(z + 8 - i, 8) * HALF, HALF), HALF)
        part = lax.dot_general(cots[i], ow_v[:, cols], CONTRACT, preferred_element_type=F32)
        dn[...] = part if i == 0 else dn[...] + part
    for c in sends:
        c.wait()
    got = [yslot_f[lax.rem(y + 4 - i, 4)] for i in range(4)]
    p1 = got[0]
    p2 = compose(got[1], p1)
    p3 = compose(got[2], p2)
    total = compose(got[3], p3)
    xslot_f[0] = total
    sends = [
        send(xslot_f.at[0], xslot_f.at[d], sems_f, 3 + d, at(lax.rem(x + d, 4), y, core))
        for d in (1, 2, 3)
    ]
    for c in sends:
        c.start()
    before = jnp.where(y == 1, p1, jnp.where(y == 2, p2, p3))
    for i in range(2):
        msave_i[i] = cslot[i, :, :DK]
    for i in range(4):
        msave_i[2 + i] = got[i][:, :DK]
    for c in sends:
        c.wait()
    gx = [xslot_f[lax.rem(x + 4 - i, 4)] for i in range(4)]
    for i in range(4):
        msave_i[6 + i] = gx[i][:, :DK]
    s1 = gx[0][:, DK:]
    s2 = mm(gx[1][:, :DK], s1) + gx[1][:, DK:]
    s3 = mm(gx[2][:, :DK], s2) + gx[2][:, DK:]
    group = jnp.where(x == 0, 0.0, jnp.where(x == 1, s1, jnp.where(x == 2, s2, s3)))
    s_chip = jnp.where(y == 0, group, mm(before[:, :DK], group) + before[:, DK:])
    s_next = mm(first[:, :DK], s_chip) + first[:, DK:]
    fin_f[2] = jnp.where(core == 0, s_next, s_chip)
    c1 = send(fin_f.at[2], fin_f.at[core], sems_f, 7, at(x, y, 1 - core))
    c1.start()
    fin_f[core] = jnp.where(core == 0, s_chip, s_next)
    c1.wait()
    start_i[0] = fin_f[0]
    start_i[1] = fin_f[1]


    for h in range(heads):
        esum[h] = jnp.zeros((DK, DK), F32)

    def forward(step, carry):
        jobs = [(h, 2 * step + cc) for cc in range(2) for h in range(heads)]
        starts = [rhs(start_i[h]) for h in range(heads)]
        states = [
            pmm(lhs(pm_i[h, crows(c), :]), starts[h]) + po_i[h, crows(c), :] for h, c in jobs
        ]
        s4 = [rhs(s) for s in states]
        wq = [
            pmm(lhs(jnp.concatenate([w_i[h, crows(c), :], q_i[h, trows(c), :]], axis=0)), b)
            for (h, c), b in zip(jobs, s4)
        ]
        us = [uv_i[h, crows(c), :] - r[:CR] for (h, c), r in zip(jobs, wq)]
        outs = [r[CR:] + mm(a_i[h, trows(c), :], u) for (h, c), r, u in zip(jobs, wq, us)]
        dos = []
        for (h, c), s, u, o in zip(jobs, states, us, outs):
            g = gain[h : h + 1, :]
            r = lax.rsqrt(jnp.mean(o * o, axis=1, keepdims=True) + 1e-5)
            normed[trows(c), h * DK : (h + 1) * DK] = (o * r * g).astype(BF16)
            dy = dn[trows(c), h * DK : (h + 1) * DK] * g
            back = jnp.mean(o * dy, axis=1, keepdims=True)
            do = r * (dy - o * (r * r * back))
            dos.append(do)
            s_s[h, crows(c), :] = s
            u_s[h, crows(c), :] = u
            do_s[h, trows(c), :] = do
        ys = [mmt(a_i[h, trows(c), :], do) for (h, c), do in zip(jobs, dos)]
        es = [
            mmt(q_i[h, trows(c), :], do) - mmt(w_i[h, crows(c), :], yy)
            for (h, c), do, yy in zip(jobs, dos, ys)
        ]
        adds = [mmt(pm_i[h, crows(c), :], e) for (h, c), e in zip(jobs, es)]
        for (h, c), yy, e, add in zip(jobs, ys, es, adds):
            y_s[h, crows(c), :] = yy
            e_s[h, crows(c), :] = e
            esum[h] += add
        return carry

    lax.fori_loop(0, chunks // 2, forward, 0)

    def mixed_term(dest, j):
        cols = pl.ds(pl.multiple_of(dest * HALF, HALF), HALF)
        return jnp.dot(
            normed[j * HALF : (j + 1) * HALF, :], ow_v[:, cols], preferred_element_type=F32
        )

    mixed = Scatter(mixed_term, mixed_o, msent, mcame, sems_m, z)
    c0 = send(esum.at[1 - core], ec.at[core], sems_b, 0, at(x, y, 1 - core))
    c0.start()
    for j in (0, 1):
        for way in (RIGHT, LEFT):
            mixed.step(way, 0, j)
            if j != way:
                mixed.step(way, 1, j)
    ec[core] = esum[core]
    c0.wait()
    e1 = ec[1]
    yslot_b[0] = mmt(msave_i[0], e1) + ec[0]
    sends = [
        send(yslot_b.at[0], yslot_b.at[d], sems_b, d, at(x, lax.rem(y + d, 4), core)) for d in (1, 2, 3)
    ]
    for c in sends:
        c.start()
    my = [msave_i[2 + i] for i in range(4)]
    suf1 = mm(my[3], my[2])
    suf0 = mm(suf1, my[1])
    for way in (RIGHT, LEFT):
        mixed.step(way, 1, way)
    suf = jnp.where(y == 2, my[3], jnp.where(y == 1, suf1, suf0))
    for c in sends:
        c.wait()
    got = [yslot_b[lax.rem(y + 4 - i, 4)] for i in range(4)]
    r3 = got[3]
    r2 = mmt(my[2], r3) + got[2]
    r1 = mmt(my[1], r2) + got[1]
    xslot_b[0] = mmt(my[0], r1) + got[0]
    sends = [
        send(xslot_b.at[0], xslot_b.at[d], sems_b, 3 + d, at(lax.rem(x + d, 4), y, core))
        for d in (1, 2, 3)
    ]
    for c in sends:
        c.start()
    for j in (0, 1):
        for way in (RIGHT, LEFT):
            mixed.step(way, 2, way if j else 1 - way)
    inside = jnp.where(y == 2, r3, jnp.where(y == 1, r2, r1))
    for c in sends:
        c.wait()
    gx = [xslot_b[lax.rem(x + 4 - i, 4)] for i in range(4)]
    x2 = gx[3]
    x1 = mmt(msave_i[8], x2) + gx[2]
    x0 = mmt(msave_i[7], x1) + gx[1]
    group = jnp.where(x == 3, 0.0, jnp.where(x == 2, x2, jnp.where(x == 1, x1, x0)))
    d_chip = jnp.where(y == 3, group, mmt(suf, group) + inside)
    d_prev = mmt(msave_i[1], d_chip) + e1
    fin_b[2] = jnp.where(core == 1, d_prev, d_chip)
    c1 = send(fin_b.at[2], fin_b.at[core], sems_b, 7, at(x, y, 1 - core))
    c1.start()
    fin_b[core] = jnp.where(core == 1, d_chip, d_prev)
    c1.wait()

    def chain(step, carry):
        c = chunks - 1 - step
        for h in range(heads):
            cur = fin_b[h]
            d_s[h, crows(c), :] = cur
            fin_b[h] = mmt(mc_i[h, crows(c), :], cur) + e_s[h, crows(c), :]
        return carry

    lax.fori_loop(0, chunks, chain, 0)

    for j in (0, 1):
        for way in (RIGHT, LEFT):
            mixed.step(way, 3, way if j else 1 - way)

    def grad_term(dest, j):
        rows = slice(j * HALF, (j + 1) * HALF)
        part = pl.ds(pl.multiple_of(dest * HALF, HALF), HALF)
        return lax.dot_general(
            gproj[rows, :], pw_v[part, :], CONTRACT, preferred_element_type=F32
        ) + lax.dot_general(glogit[rows, :], bw[part, :], CONTRACT, preferred_element_type=F32)

    grads = Scatter(grad_term, grad_o, gsent, gcame, sems_g, z)

    def backward(step, carry):
        r_at, c_at = orders(CR, CR, False, False)
        below = r_at > c_at
        tr, tc = orders(CT, CR, True, False)
        visible = tc <= 2 * tr + 1
        jobs = [(h, 2 * step + cc) for cc in range(2) for h in range(heads)]
        ks = [k_i[h, crows(c), :] for h, c in jobs]
        k4 = [rhs(k) for k in ks]
        ds = [d_s[h, crows(c), :] for h, c in jobs]
        us = [u_s[h, crows(c), :] for h, c in jobs]
        dus = [mm(k, d) + y_s[h, crows(c), :] for (h, c), k, d in zip(jobs, ks, ds)]
        zs = [mmt(t_i[h, crows(c), :], du) for (h, c), du in zip(jobs, dus)]
        sigs = [strengths(logit, c, h) for h, c in jobs]
        bzs = [2.0 * sg[0] * z for sg, z in zip(sigs, zs)]
        dos = [do_s[h, trows(c), :] for h, c in jobs]
        both = [lhs(jnp.concatenate([bz, do], axis=0)) for bz, do in zip(bzs, dos)]
        pus = [pmm(b2, rhs(u.T)) for b2, u in zip(both, us)]
        pss = [pmm(b2, rhs(s_s[h, crows(c), :].T)) for (h, c), b2 in zip(jobs, both)]
        pbs = [jnp.where(below, p[:CR], 0.0) for p in pus]
        das = [jnp.where(visible, p[CR:], 0.0) for p in pus]
        mixes = [
            pmm(lhs(jnp.concatenate([pb + pb.T, da], axis=0)), kk)
            for pb, da, kk in zip(pbs, das, k4)
        ]
        dks = [
            mm(u, d.T) - ps[:CR] - mx[:CR] + mmt(da, q_i[h, trows(c), :])
            for (h, c), u, d, ps, mx, da in zip(jobs, us, ds, pss, mixes, das)
        ]
        dqs = [mx[CR:] + ps[CR:] for mx, ps in zip(mixes, pss)]
        for (h, c), k, u, z, bz, sg, dk, dq in zip(jobs, ks, us, zs, bzs, sigs, dks, dqs):
            a, c1, c2, _, _ = head_rows(proj, c, h)
            q = q_i[h, trows(c), :]
            sa = unit_scale(a, 1e-6)
            sc = jnp.concatenate([unit_scale(c1, 1e-6), unit_scale(c2, 1e-6)], axis=0)
            ga = sa * (dq - q * jnp.sum(q * dq, axis=1, keepdims=True))
            gc = sc * (dk - k * jnp.sum(k * dk, axis=1, keepdims=True))
            base = h * 5 * DK
            gproj[trows(c), base : base + DK] = ga.astype(BF16)
            gproj[trows(c), base + DK : base + 2 * DK] = gc[:CT].astype(BF16)
            gproj[trows(c), base + 2 * DK : base + 3 * DK] = gc[CT:].astype(BF16)
            gproj[trows(c), base + 3 * DK : base + 4 * DK] = bz[:CT].astype(BF16)
            gproj[trows(c), base + 4 * DK : base + 5 * DK] = bz[CT:].astype(BF16)
            gl = jnp.sum(z * u, axis=1, keepdims=True) * sg[1]
            glogit[trows(c), 2 * h : 2 * h + 1] = gl[:CT].astype(BF16)
            glogit[trows(c), 2 * h + 1 : 2 * h + 2] = gl[CT:].astype(BF16)
        return carry

    lax.fori_loop(0, chunks // 2, backward, 0)
    mixed.finish()
    for j in (0, 1):
        for way in (RIGHT, LEFT):
            grads.step(way, 0, j)
            if j != way:
                grads.step(way, 1, j)
    for way in (RIGHT, LEFT):
        grads.step(way, 1, way)
    for s in (2, 3):
        for j in (0, 1):
            for way in (RIGHT, LEFT):
                grads.step(way, s, way if j else 1 - way)
    grads.finish()
    gather_end(hids, sems_h, z)
    gather_end(cots, sems_c, z)


def params(collective_id, mib):
    return pltpu.CompilerParams(
        collective_id=collective_id, has_side_effects=True, vmem_limit_bytes=mib << 20
    )


def local(hidden_in, proj_weight, beta_weight, norm_gain, out_weight, cotangent):
    rows = hidden_in.shape[0]
    buf = lambda *shape: pltpu.VMEM(shape, F32)
    low = lambda *shape: pltpu.VMEM(shape, BF16)
    dma = lambda *shape: pltpu.SemaphoreType.DMA(shape)
    part, full = buf(2, rows, DK), buf(2, REFL * rows, DK)
    square, slots = buf(2, DK, DK), buf(4, DK, DK)
    wide, wide_slots = buf(2, DK, 2 * DK), buf(4, DK, 2 * DK)
    out = jax.ShapeDtypeStruct((rows, HALF), BF16)
    anywhere = pl.BlockSpec(memory_space=pl.ANY)
    return pl.pallas_call(
        layer_kernel,
        out_shape=[out, out],
        in_specs=[VM, anywhere, VM, VM, anywhere, VM],
        out_specs=[VM, VM],
        scratch_shapes=[
            low(8, rows, HALF), low(8, rows, HALF), low(*proj_weight.shape), low(*out_weight.shape),
            buf(rows, proj_weight.shape[1]), buf(rows, 4), buf(rows, 2 * DK),
            part, full, full, full, full, part, full, full, full, square, buf(10, DK, DK),
            full, wide, wide, wide_slots, wide_slots, buf(3, DK, DK),
            full, full, part, full, full, full, square, square, slots, slots, buf(3, DK, DK),
            low(rows, 2 * DK), low(rows, 10 * DK), low(rows, 4),
            low(2, 4, rows, HALF), low(2, 4, rows, HALF),
            low(2, 4, rows, HALF), low(2, 4, rows, HALF),
            dma(2, 2, 4, 2), dma(2, 2, 4, 2), dma(2, 8), dma(2, 8),
            dma(2, 2, 4, 2), dma(2, 2, 4, 2), dma(2),
        ],
        compiler_params=params(1, 60),
    )(hidden_in, proj_weight, beta_weight, norm_gain.reshape(2, DK), out_weight, cotangent)


def solution(mesh):
    placed = (
        P("seq", "head"),
        P(None, "head"),
        P(None, "head"),
        P("head"),
        P("head", None),
        P("seq", "head"),
    )
    return jax.shard_map(
        local,
        mesh=mesh,
        in_specs=placed,
        out_specs=(P("seq", "head"), P("seq", "head")),
        check_vma=False,
    )
```

```python
import jax
import jax.numpy as jnp
from jax import lax
from jax.experimental import pallas as pl
from jax.experimental.pallas import tpu as pltpu
from jax.sharding import PartitionSpec as P

DK = 128
REFL = 2
CT = 64
CR = CT * REFL
MESH = pl.DeviceIdType.MESH
F32 = jnp.float32
BF16 = jnp.bfloat16
VM = pl.BlockSpec(memory_space=pltpu.VMEM)


def split(a):
    hi = a.astype(BF16)
    lo = (a - hi.astype(F32)).astype(BF16)
    return hi, lo


def lhs(a):
    hi, lo = split(a)
    return jnp.concatenate([hi, lo], axis=1)


def rhs(b):
    hi, lo = split(b)
    row = jnp.concatenate([hi, lo], axis=1)
    return jnp.concatenate([row, row], axis=0)


def pmm(a2, b4):
    n = b4.shape[1] // 2
    r = jnp.dot(a2, b4, preferred_element_type=F32)
    return r[:, :n] + r[:, n:]


def mm(a, b):
    return pmm(lhs(a), rhs(b))


def mmt(a, b):
    return pmm(lhs(a.T), rhs(b))


def mmb(a, b):
    hi, lo = split(b)
    n = b.shape[1]
    r = jnp.dot(a, jnp.concatenate([hi, lo], axis=1), preferred_element_type=F32)
    return r[:, :n] + r[:, n:]


def orders(rows, cols, row_tokens, col_tokens):
    r = lax.broadcasted_iota(jnp.int32, (rows, cols), 0)
    c = lax.broadcasted_iota(jnp.int32, (rows, cols), 1)
    if row_tokens:
        r_at = r
    else:
        r_at = 2 * (r % CT) + r // CT
    c_at = 2 * (c % CT) + c // CT
    return r_at, c_at


def unit_scale(v, eps):
    return lax.rsqrt(jnp.sum(v * v, axis=1, keepdims=True) + eps)


def head_rows(proj_ref, c, h):
    rows = pl.ds(pl.multiple_of(c * CT, CT), CT)
    base = h * 5 * DK
    return [proj_ref[rows, base + i * DK : base + (i + 1) * DK] for i in range(5)]


def strengths(logit_ref, c, h):
    rows = pl.ds(pl.multiple_of(c * CT, CT), CT)
    x = jnp.concatenate(
        [logit_ref[rows, 2 * h : 2 * h + 1], logit_ref[rows, 2 * h + 1 : 2 * h + 2]], axis=0
    )
    return 1.0 / (1.0 + jnp.exp(-x)), 1.0 / (1.0 + jnp.exp(x))


def crows(c):
    return pl.ds(pl.multiple_of(c * CR, CR), CR)


def trows(c):
    return pl.ds(pl.multiple_of(c * CT, CT), CT)


def place():
    s = lax.axis_index("seq")
    core = lax.rem(s, 2)
    y = lax.rem(lax.div(s, 2), 4)
    x = lax.div(s, 8)
    return x, y, core


def at(x, y, core):
    return (x * 4 + y) * 2 + core


def meet(x, y, core, z):
    barrier = pltpu.get_barrier_semaphore()
    peers = [{"seq": at(x, y, 1 - core)}]
    for d in (1, 2, 3):
        peers.append({"seq": at(x, lax.rem(y + d, 4), core)})
        peers.append({"seq": at(lax.rem(x + d, 4), y, core)})
    peers.append({"head": lax.rem(z + 1, 8)})
    peers.append({"head": lax.rem(z + 7, 8)})
    for p in peers:
        pl.semaphore_signal(barrier, inc=1, device_id=p, device_id_type=MESH)
    pl.semaphore_wait(barrier, len(peers))


RIGHT, LEFT = 0, 1
HALF = 256


def beside(z, way):
    return {"head": lax.rem(z + (1 if way == RIGHT else 7), 8)}


def gather_unit(buf, sems, z, way, d, j):
    src, dst = (d - 1, d) if way == RIGHT else ((9 - d) % 8, 8 - d)
    rows = pl.ds(j * HALF, HALF)
    return pltpu.make_async_remote_copy(
        src_ref=buf.at[src, rows],
        dst_ref=buf.at[dst, rows],
        send_sem=sems.at[0, way, d - 1, j],
        recv_sem=sems.at[1, way, d - 1, j],
        device_id=beside(z, way),
        device_id_type=MESH,
    )


def gather_has(way, d, j):
    return d < 4 or (d == 4 and j == way)


def gather_start(buf, sems, z):
    for j in (0, 1):
        for way in (RIGHT, LEFT):
            gather_unit(buf, sems, z, way, 1, j).start()


def gather_step(buf, sems, z, d):
    for j in (0, 1):
        for way in (RIGHT, LEFT):
            if gather_has(way, d, j):
                gather_unit(buf, sems, z, way, d, j).wait_recv()
                if gather_has(way, d + 1, j):
                    gather_unit(buf, sems, z, way, d + 1, j).start()


def gather_end(buf, sems, z):
    for d in (1, 2, 3, 4):
        for j in (0, 1):
            for way in (RIGHT, LEFT):
                if gather_has(way, d, j):
                    gather_unit(buf, sems, z, way, d, j).wait_send()


class Scatter:
    def __init__(self, own, out, col, sent, came, sems, z):
        self.own, self.out, self.col, self.z = own, out, col, z
        self.sent, self.came, self.sems = sent, came, sems

    def unit(self, way, s, j):
        rows = pl.ds(j * HALF, HALF)
        return pltpu.make_async_remote_copy(
            src_ref=self.sent.at[way, s, rows],
            dst_ref=self.came.at[way, s, rows],
            send_sem=self.sems.at[0, way, s, j],
            recv_sem=self.sems.at[1, way, s, j],
            device_id=beside(self.z, way),
            device_id_type=MESH,
        )

    def has(self, way, s, j):
        return s > 0 or j == way

    def step(self, way, s, j):
        if not self.has(way, s, j):
            return
        rows = slice(j * HALF, (j + 1) * HALF)
        dest = lax.rem(self.z + ((4 - s) if way == RIGHT else (4 + s)), 8)
        term = self.own(dest, j)
        if s > 0 and self.has(way, s - 1, j):
            self.unit(way, s - 1, j).wait_recv()
            term = term + self.came[way, s - 1, rows].astype(F32)
        self.sent[way, s, rows] = term.astype(BF16)
        self.unit(way, s, j).start()

    def finish(self, j):
        rows = slice(j * HALF, (j + 1) * HALF)
        term = self.own(self.z, j)
        for way in (RIGHT, LEFT):
            self.unit(way, 3, j).wait_recv()
            term = term + self.came[way, 3, rows].astype(F32)
        self.out[rows, self.col : self.col + HALF] = term.astype(BF16)

    def end(self):
        for way in (RIGHT, LEFT):
            for s in range(4):
                for j in (0, 1):
                    if self.has(way, s, j):
                        self.unit(way, s, j).wait_send()


def send(src, dst, sems, i, seq):
    return pltpu.make_async_remote_copy(
        src_ref=src,
        dst_ref=dst,
        send_sem=sems.at[0, i],
        recv_sem=sems.at[1, i],
        device_id={"seq": seq},
        device_id_type=MESH,
    )


def compose(later, earlier, times=mm):
    r = times(later[:, :DK], earlier)
    return jnp.concatenate([r[:, :DK], r[:, DK:] + later[:, DK:].astype(F32)], axis=1)


def eye_nat():
    r = lax.broadcasted_iota(jnp.int32, (DK, DK), 0)
    c = lax.broadcasted_iota(jnp.int32, (DK, DK), 1)
    return jnp.where(r == c, 1.0, 0.0)


CONTRACT = (((1,), (1,)), ((), ()))


def layer_kernel(
    hid, pw, bw, gain, ow, cot,
    out,
    hids, cots, pw_v, ow_v, proj, logit, dn,
    q_i, k_i, w_i, uv_i, t_i, a_i, pm_i, po_i, mc_i, msave, qp_s, q2_s, o2_s,
    oc, mo, cslot, yslot_f, xslot_f, fin_f,
    s_s, u_s, do_s, y_s, e_s, d_s, esum, ec, yslot_b, xslot_b, fin_b,
    normed, gproj, glogit, msent, mcame, gsent, gcame,
    sems_h, sems_c, sems_f, sems_b, sems_m, sems_g, sems_w,
):
    heads = 2
    chunks = proj.shape[0] // CT
    x, y, core = place()
    z = lax.axis_index("head")
    pw_copy = pltpu.make_async_copy(pw, pw_v, sems_w.at[0])
    ow_copy = pltpu.make_async_copy(ow, ow_v, sems_w.at[1])
    pw_copy.start()
    ow_copy.start()
    hids[0] = hid[...]
    cots[0] = cot[...]
    meet(x, y, core, z)

    gather_start(hids, sems_h, z)
    pw_copy.wait()
    for d in range(5):
        if d > 0:
            gather_step(hids, sems_h, z, d)
        if d == 3:
            gather_start(cots, sems_c, z)
        for i in {d, (8 - d) % 8}:
            rows = pl.ds(pl.multiple_of(lax.rem(z + 8 - i, 8) * HALF, HALF), HALF)
            part = jnp.dot(hids[i], pw_v[rows, :], preferred_element_type=F32)
            part_b = lax.dot_general(hids[i], bw[:, rows], CONTRACT, preferred_element_type=F32)
            proj[...] = part if i == 0 else proj[...] + part
            logit[...] = part_b if i == 0 else logit[...] + part_b

    def chunk_pair(step, carry):
        for d in (1, 2, 3):
            pl.when(step == d)(lambda d=d: gather_step(cots, sems_c, z, d))
        r_at, c_at = orders(CR, CR, False, False)
        below = r_at > c_at
        diff = jnp.bitwise_xor(r_at, c_at)
        tr, tc = orders(CT, CR, True, False)
        visible = tc <= 2 * tr + 1
        eye = jnp.where(r_at == c_at, 1.0, 0.0)
        jobs = [(h, 2 * step + cc) for cc in range(2) for h in range(heads)]
        ks, bs, vs, qs = [], [], [], []
        for h, c in jobs:
            a, c1, c2, v1, v2 = head_rows(proj, c, h)
            q = a * unit_scale(a, 1e-6)
            k = jnp.concatenate([c1 * unit_scale(c1, 1e-6), c2 * unit_scale(c2, 1e-6)], axis=0)
            sig, _ = strengths(logit, c, h)
            ks.append(k)
            qs.append(q)
            bs.append(2.0 * sig)
            vs.append(jnp.concatenate([v1, v2], axis=0))
            q_i[h, trows(c), :] = q
            k_i[h, crows(c), :] = k
        kts = [k.T for k in ks]
        kt4 = [rhs(kt) for kt in kts]
        grams = [pmm(lhs(jnp.concatenate([k, q], axis=0)), b4) for k, q, b4 in zip(ks, qs, kt4)]
        for (h, c), g in zip(jobs, grams):
            a_i[h, trows(c), :] = jnp.where(visible, g[CR:], 0.0)
        ns = [jnp.where(below, b * g[:CR], 0.0) for b, g in zip(bs, grams)]
        ts = [eye - jnp.where(diff == 1, n, 0.0) for n in ns]
        level = 1
        while (1 << level) < CR:
            parts = [jnp.where((diff >> level) == 1, n, 0.0) for n in ns]
            inner = [mm(p, t) for p, t in zip(parts, ts)]
            outer = [mm(t, i) for t, i in zip(ts, inner)]
            ts = [t - o for t, o in zip(ts, outer)]
            level += 1
        wus = [mm(t, b * jnp.concatenate([k, v], axis=1)) for t, b, k, v in zip(ts, bs, ks, vs)]
        mos = [pmm(lhs(kt), rhs(wu)) for kt, wu in zip(kts, wus)]
        for (h, c), t, wu, m in zip(jobs, ts, wus, mos):
            t_i[h, crows(c), :] = t
            w_i[h, crows(c), :] = wu[:, :DK]
            uv_i[h, crows(c), :] = wu[:, DK:]
            mc_i[h, crows(c), :] = eye_nat() - m[:, :DK]
            oc[h, crows(c), :] = m[:, DK:]
        return carry

    lax.fori_loop(0, chunks // 2, chunk_pair, 0)

    for h in range(heads):
        mo[h, :, :DK] = eye_nat()
        mo[h, :, DK:] = jnp.zeros((DK, DK), F32)

    def prefix(c, carry):
        for h in range(heads):
            cur = mo[h]
            pm_i[h, crows(c), :] = cur[:, :DK]
            po_i[h, crows(c), :] = cur[:, DK:]
            r = mm(mc_i[h, crows(c), :], cur)
            mo[h, :, :DK] = r[:, :DK]
            mo[h, :, DK:] = r[:, DK:] + oc[h, crows(c), :]
        return carry

    lax.fori_loop(0, chunks, prefix, 0)

    c0 = send(mo.at[1 - core], cslot.at[core], sems_f, 0, at(x, y, 1 - core))
    c0.start()
    cslot[core] = mo[core]
    c0.wait()
    first = cslot[0]
    yslot_f[0] = compose(cslot[1], first).astype(BF16)
    sends = [
        send(yslot_f.at[0], yslot_f.at[d], sems_f, d, at(x, lax.rem(y + d, 4), core))
        for d in (1, 2, 3)
    ]
    for c in sends:
        c.start()

    def read_maps(step, carry):
        jobs = [(h, 2 * step + cc) for cc in range(2) for h in range(heads)]
        sees = [lhs(a_i[h, trows(c), :]) for h, c in jobs]
        aws = [pmm(a2, rhs(w_i[h, crows(c), :])) for (h, c), a2 in zip(jobs, sees)]
        aus = [pmm(a2, rhs(uv_i[h, crows(c), :])) for (h, c), a2 in zip(jobs, sees)]
        qps = [q_i[h, trows(c), :] - aw for (h, c), aw in zip(jobs, aws)]
        qp2 = [lhs(qp) for qp in qps]
        q2s = [pmm(a2, rhs(pm_i[h, crows(c), :])) for (h, c), a2 in zip(jobs, qp2)]
        o2s = [pmm(a2, rhs(po_i[h, crows(c), :])) for (h, c), a2 in zip(jobs, qp2)]
        for (h, c), qp, q2, o2, au in zip(jobs, qps, q2s, o2s, aus):
            qp_s[h, trows(c), :] = qp
            q2_s[h, trows(c), :] = q2
            o2_s[h, trows(c), :] = o2 + au
        return carry

    lax.fori_loop(0, chunks // 2, read_maps, 0)
    for c in sends:
        c.wait()
    got = [yslot_f[lax.rem(y + 4 - i, 4)] for i in range(4)]
    p1 = got[0].astype(F32)
    p2 = compose(got[1], p1, mmb)
    p3 = compose(got[2], p2, mmb)
    xslot_f[0] = compose(got[3], p3, mmb).astype(BF16)
    sends = [
        send(xslot_f.at[0], xslot_f.at[d], sems_f, 3 + d, at(lax.rem(x + d, 4), y, core))
        for d in (1, 2, 3)
    ]
    for c in sends:
        c.start()
    before = jnp.where(y == 1, p1, jnp.where(y == 2, p2, p3))
    m_y = [g[:, :DK].T for g in got]
    suf1 = mmb(m_y[2], m_y[3].astype(F32))
    suf0 = mmb(m_y[1], suf1)
    suf = jnp.where(y == 2, m_y[3].astype(F32), jnp.where(y == 1, suf1, suf0))
    for i in range(4):
        msave[i] = m_y[i]
    gather_step(cots, sems_c, z, 4)
    ow_copy.wait()
    for i in range(8):
        cols = pl.ds(pl.multiple_of(lax.rem(z + 8 - i, 8) * HALF, HALF), HALF)
        term = lax.dot_general(cots[i], ow_v[:, cols], CONTRACT, preferred_element_type=F32)
        dn[...] = term if i == 0 else dn[...] + term
    for c in sends:
        c.wait()
    gx = [xslot_f[lax.rem(x + 4 - i, 4)] for i in range(4)]
    s1 = gx[0][:, DK:].astype(F32)
    s2 = mmb(gx[1][:, :DK], s1) + gx[1][:, DK:].astype(F32)
    s3 = mmb(gx[2][:, :DK], s2) + gx[2][:, DK:].astype(F32)
    group = jnp.where(x == 0, 0.0, jnp.where(x == 1, s1, jnp.where(x == 2, s2, s3)))
    s_chip = jnp.where(y == 0, group, mm(before[:, :DK], group) + before[:, DK:])
    s_next = mm(first[:, :DK], s_chip) + first[:, DK:]
    fin_f[2] = jnp.where(core == 0, s_next, s_chip)
    c1 = send(fin_f.at[2], fin_f.at[core], sems_f, 7, at(x, y, 1 - core))
    c1.start()
    fin_f[core] = jnp.where(core == 0, s_chip, s_next)
    c1.wait()

    outs, scales = [], []
    for h in range(heads):
        o = mm(q2_s[h], fin_f[h]) + o2_s[h]
        r = lax.rsqrt(jnp.mean(o * o, axis=1, keepdims=True) + 1e-5)
        normed[:, h * DK : (h + 1) * DK] = (o * r * gain[h : h + 1, :]).astype(BF16)
        outs.append(o)
        scales.append(r)

    def mixed_term(dest, j):
        cols = pl.ds(pl.multiple_of(dest * HALF, HALF), HALF)
        return jnp.dot(
            normed[j * HALF : (j + 1) * HALF, :], ow_v[:, cols], preferred_element_type=F32
        )

    mixed = Scatter(mixed_term, out, 0, msent, mcame, sems_m, z)
    mixed.step(RIGHT, 0, 0)
    mixed.step(LEFT, 0, 1)
    mixed.step(RIGHT, 1, 1)
    mixed.step(LEFT, 1, 0)
    for h in range(heads):
        o, r = outs[h], scales[h]
        dy = dn[:, h * DK : (h + 1) * DK] * gain[h : h + 1, :]
        back = jnp.mean(o * dy, axis=1, keepdims=True)
        do = r * (dy - o * (r * r * back))
        do_s[h] = do
        esum[h] = mmt(q2_s[h], do)

    c0 = send(esum.at[1 - core], ec.at[core], sems_b, 0, at(x, y, 1 - core))
    c0.start()
    ec[core] = esum[core]
    m_c = [cslot[i, :, :DK].T for i in range(2)]
    c0.wait()
    e1 = ec[1]
    yslot_b[0] = (mm(m_c[0], e1) + ec[0]).astype(BF16)
    sends = [
        send(yslot_b.at[0], yslot_b.at[d], sems_b, d, at(x, lax.rem(y + d, 4), core))
        for d in (1, 2, 3)
    ]
    for c in sends:
        c.start()

    def inner_parts(step, carry):
        @pl.when(step == 1)
        def _():
            mixed.step(RIGHT, 1, 0)
            mixed.step(LEFT, 1, 1)

        @pl.when(step == 3)
        def _():
            mixed.step(RIGHT, 2, 1)
            mixed.step(LEFT, 2, 0)

        jobs = [(h, 2 * step + cc) for cc in range(2) for h in range(heads)]
        starts = [rhs(fin_f[h]) for h in range(heads)]
        states = [
            pmm(lhs(pm_i[h, crows(c), :]), starts[h]) + po_i[h, crows(c), :] for h, c in jobs
        ]
        us = [uv_i[h, crows(c), :] - mm(w_i[h, crows(c), :], s) for (h, c), s in zip(jobs, states)]
        dos = [do_s[h, trows(c), :] for h, c in jobs]
        sides = [
            mmt(jnp.concatenate([a_i[h, trows(c), :], qp_s[h, trows(c), :]], axis=1), do)
            for (h, c), do in zip(jobs, dos)
        ]
        for (h, c), s, u, side in zip(jobs, states, us, sides):
            s_s[h, crows(c), :] = s
            u_s[h, crows(c), :] = u
            y_s[h, crows(c), :] = side[:CR]
            e_s[h, crows(c), :] = side[CR:]
        return carry

    lax.fori_loop(0, chunks // 2, inner_parts, 0)
    for c in sends:
        c.wait()
    got = [yslot_b[lax.rem(y + 4 - i, 4)] for i in range(4)]
    r3 = got[3].astype(F32)
    r2 = mmb(msave[2], r3) + got[2].astype(F32)
    r1 = mmb(msave[1], r2) + got[1].astype(F32)
    xslot_b[0] = (mmb(msave[0], r1) + got[0].astype(F32)).astype(BF16)
    sends = [
        send(xslot_b.at[0], xslot_b.at[d], sems_b, 3 + d, at(lax.rem(x + d, 4), y, core))
        for d in (1, 2, 3)
    ]
    for c in sends:
        c.start()
    inside = jnp.where(y == 2, r3, jnp.where(y == 1, r2, r1))
    m_x = [xslot_f[lax.rem(x + 4 - i, 4), :, :DK].T for i in (1, 2)]
    mixed.step(RIGHT, 2, 0)
    mixed.step(LEFT, 2, 1)
    for c in sends:
        c.wait()
    gx = [xslot_b[lax.rem(x + 4 - i, 4)].astype(F32) for i in range(4)]
    x2 = gx[3]
    x1 = mmb(m_x[1], x2) + gx[2]
    x0 = mmb(m_x[0], x1) + gx[1]
    group = jnp.where(x == 3, 0.0, jnp.where(x == 2, x2, jnp.where(x == 1, x1, x0)))
    d_chip = jnp.where(y == 3, group, mm(suf, group) + inside)
    d_prev = mm(m_c[1], d_chip) + e1
    fin_b[2] = jnp.where(core == 1, d_prev, d_chip)
    c1 = send(fin_b.at[2], fin_b.at[core], sems_b, 7, at(x, y, 1 - core))
    c1.start()
    fin_b[core] = jnp.where(core == 1, d_chip, d_prev)
    mixed.step(RIGHT, 3, 1)
    mixed.step(LEFT, 3, 0)
    c1.wait()

    def chain(step, carry):
        c = chunks - 1 - step
        for h in range(heads):
            cur = fin_b[h]
            d_s[h, crows(c), :] = cur
            fin_b[h] = mmt(mc_i[h, crows(c), :], cur) + e_s[h, crows(c), :]
        return carry

    lax.fori_loop(0, chunks, chain, 0)

    def grad_term(dest, j):
        rows = slice(j * HALF, (j + 1) * HALF)
        part = pl.ds(pl.multiple_of(dest * HALF, HALF), HALF)
        return lax.dot_general(
            gproj[rows, :], pw_v[part, :], CONTRACT, preferred_element_type=F32
        ) + jnp.dot(glogit[rows, :], bw[:, part], preferred_element_type=F32)

    grads = Scatter(grad_term, out, HALF, gsent, gcame, sems_g, z)

    def backward(step, carry):
        @pl.when(step == 1)
        def _():
            mixed.step(RIGHT, 3, 0)
            mixed.step(LEFT, 3, 1)

        @pl.when(step == 2)
        def _():
            grads.step(RIGHT, 0, 0)
            grads.step(LEFT, 1, 0)

        @pl.when(step == 3)
        def _():
            grads.step(RIGHT, 1, 0)
            grads.step(LEFT, 2, 0)

        r_at, c_at = orders(CR, CR, False, False)
        below = r_at > c_at
        tr, tc = orders(CT, CR, True, False)
        visible = tc <= 2 * tr + 1
        jobs = [(h, 2 * step + cc) for cc in range(2) for h in range(heads)]
        ks = [k_i[h, crows(c), :] for h, c in jobs]
        k4 = [rhs(k) for k in ks]
        ds = [d_s[h, crows(c), :] for h, c in jobs]
        us = [u_s[h, crows(c), :] for h, c in jobs]
        dus = [mm(k, d) + y_s[h, crows(c), :] for (h, c), k, d in zip(jobs, ks, ds)]
        zs = [mmt(t_i[h, crows(c), :], du) for (h, c), du in zip(jobs, dus)]
        sigs = [strengths(logit, c, h) for h, c in jobs]
        bzs = [2.0 * sg[0] * z for sg, z in zip(sigs, zs)]
        dos = [do_s[h, trows(c), :] for h, c in jobs]
        both = [lhs(jnp.concatenate([bz, do], axis=0)) for bz, do in zip(bzs, dos)]
        pus = [pmm(b2, rhs(u.T)) for b2, u in zip(both, us)]
        pss = [pmm(b2, rhs(s_s[h, crows(c), :].T)) for (h, c), b2 in zip(jobs, both)]
        pbs = [jnp.where(below, p[:CR], 0.0) for p in pus]
        das = [jnp.where(visible, p[CR:], 0.0) for p in pus]
        mixes = [
            pmm(lhs(jnp.concatenate([pb + pb.T, da], axis=0)), kk)
            for pb, da, kk in zip(pbs, das, k4)
        ]
        dks = [
            mm(u, d.T) - ps[:CR] - mx[:CR] + mmt(da, q_i[h, trows(c), :])
            for (h, c), u, d, ps, mx, da in zip(jobs, us, ds, pss, mixes, das)
        ]
        dqs = [mx[CR:] + ps[CR:] for mx, ps in zip(mixes, pss)]
        for (h, c), k, u, z, bz, sg, dk, dq in zip(jobs, ks, us, zs, bzs, sigs, dks, dqs):
            a, c1, c2, _, _ = head_rows(proj, c, h)
            q = q_i[h, trows(c), :]
            sa = unit_scale(a, 1e-6)
            sc = jnp.concatenate([unit_scale(c1, 1e-6), unit_scale(c2, 1e-6)], axis=0)
            ga = sa * (dq - q * jnp.sum(q * dq, axis=1, keepdims=True))
            gc = sc * (dk - k * jnp.sum(k * dk, axis=1, keepdims=True))
            base = h * 5 * DK
            gproj[trows(c), base : base + DK] = ga.astype(BF16)
            gproj[trows(c), base + DK : base + 2 * DK] = gc[:CT].astype(BF16)
            gproj[trows(c), base + 2 * DK : base + 3 * DK] = gc[CT:].astype(BF16)
            gproj[trows(c), base + 3 * DK : base + 4 * DK] = bz[:CT].astype(BF16)
            gproj[trows(c), base + 4 * DK : base + 5 * DK] = bz[CT:].astype(BF16)
            gl = jnp.sum(z * u, axis=1, keepdims=True) * sg[1]
            glogit[trows(c), 2 * h : 2 * h + 1] = gl[:CT].astype(BF16)
            glogit[trows(c), 2 * h + 1 : 2 * h + 2] = gl[CT:].astype(BF16)
        return carry

    lax.fori_loop(0, chunks // 2, backward, 0)
    mixed.finish(0)
    mixed.finish(1)
    grads.step(RIGHT, 1, 1)
    grads.step(LEFT, 0, 1)
    grads.step(RIGHT, 2, 0)
    grads.step(LEFT, 3, 0)
    grads.step(RIGHT, 2, 1)
    grads.step(LEFT, 1, 1)
    grads.step(RIGHT, 3, 0)
    grads.step(LEFT, 2, 1)
    grads.step(RIGHT, 3, 1)
    grads.step(LEFT, 3, 1)
    grads.finish(0)
    grads.finish(1)
    mixed.end()
    grads.end()
    gather_end(hids, sems_h, z)
    gather_end(cots, sems_c, z)


def params(collective_id, mib):
    return pltpu.CompilerParams(
        collective_id=collective_id, has_side_effects=True, vmem_limit_bytes=mib << 20
    )


def local(hidden_in, proj_weight, beta_weight, norm_gain, out_weight, cotangent):
    rows = hidden_in.shape[0]
    buf = lambda *shape: pltpu.VMEM(shape, F32)
    low = lambda *shape: pltpu.VMEM(shape, BF16)
    dma = lambda *shape: pltpu.SemaphoreType.DMA(shape)
    part, full = buf(2, rows, DK), buf(2, REFL * rows, DK)
    square, wide = buf(2, DK, DK), buf(2, DK, 2 * DK)
    anywhere = pl.BlockSpec(memory_space=pl.ANY)
    both = pl.pallas_call(
        layer_kernel,
        out_shape=jax.ShapeDtypeStruct((rows, 2 * HALF), BF16),
        in_specs=[VM, anywhere, VM, VM, anywhere, VM],
        out_specs=VM,
        scratch_shapes=[
            low(8, rows, HALF), low(8, rows, HALF), low(*proj_weight.shape), low(*out_weight.shape),
            buf(rows, proj_weight.shape[1]), buf(rows, 4), buf(rows, 2 * DK),
            part, full, full, full, full, part, full, full, full, low(4, DK, DK), part, part, part,
            full, wide, wide, low(4, DK, 2 * DK), low(4, DK, 2 * DK), buf(3, DK, DK),
            full, full, part, full, full, full, square, square, low(4, DK, DK), low(4, DK, DK), buf(3, DK, DK),
            low(rows, 2 * DK), low(rows, 10 * DK), low(rows, 4),
            low(2, 4, rows, HALF), low(2, 4, rows, HALF),
            low(2, 4, rows, HALF), low(2, 4, rows, HALF),
            dma(2, 2, 4, 2), dma(2, 2, 4, 2), dma(2, 8), dma(2, 8),
            dma(2, 2, 4, 2), dma(2, 2, 4, 2), dma(2),
        ],
        compiler_params=params(1, 60),
    )(hidden_in, proj_weight, beta_weight.T, norm_gain.reshape(2, DK), out_weight, cotangent)
    return both[:, :HALF], both[:, HALF:]


def solution(mesh):
    placed = (
        P("seq", "head"),
        P(None, "head"),
        P(None, "head"),
        P("head"),
        P("head", None),
        P("seq", "head"),
    )
    return jax.shard_map(
        local,
        mesh=mesh,
        in_specs=placed,
        out_specs=(P("seq", "head"), P("seq", "head")),
        check_vma=False,
    )
```

```python
import jax
import jax.numpy as jnp
from jax import lax
from jax.experimental import pallas as pl
from jax.experimental.pallas import tpu as pltpu
from jax.sharding import PartitionSpec as P

DK = 128
REFL = 2
CT = 64
CR = CT * REFL
BATCH = 4
MESH = pl.DeviceIdType.MESH
F32 = jnp.float32
BF16 = jnp.bfloat16
VM = pl.BlockSpec(memory_space=pltpu.VMEM)


def split(a):
    hi = a.astype(BF16)
    lo = (a - hi.astype(F32)).astype(BF16)
    return hi, lo


def lhs(a):
    hi, lo = split(a)
    return jnp.concatenate([hi, lo], axis=1)


def rhs(b):
    hi, lo = split(b)
    row = jnp.concatenate([hi, lo], axis=1)
    return jnp.concatenate([row, row], axis=0)


def pmm(a2, b4):
    n = b4.shape[1] // 2
    r = jnp.dot(a2, b4, preferred_element_type=F32)
    return r[:, :n] + r[:, n:]


def mm(a, b):
    return pmm(lhs(a), rhs(b))


def mmt(a, b):
    return pmm(lhs(a.T), rhs(b))


def mmb(a, b):
    hi, lo = split(b)
    n = b.shape[1]
    r = jnp.dot(a, jnp.concatenate([hi, lo], axis=1), preferred_element_type=F32)
    return r[:, :n] + r[:, n:]


def orders(rows, cols, row_tokens, col_tokens):
    r = lax.broadcasted_iota(jnp.int32, (rows, cols), 0)
    c = lax.broadcasted_iota(jnp.int32, (rows, cols), 1)
    if row_tokens:
        r_at = r
    else:
        r_at = 2 * (r % CT) + r // CT
    c_at = 2 * (c % CT) + c // CT
    return r_at, c_at


def unit_scale(v, eps):
    return lax.rsqrt(jnp.sum(v * v, axis=1, keepdims=True) + eps)


def head_rows(proj_ref, c, h):
    rows = pl.ds(pl.multiple_of(c * CT, CT), CT)
    base = h * 5 * DK
    return [proj_ref[rows, base + i * DK : base + (i + 1) * DK] for i in range(5)]


def strengths(logit_ref, c, h):
    rows = pl.ds(pl.multiple_of(c * CT, CT), CT)
    x = jnp.concatenate(
        [logit_ref[rows, 2 * h : 2 * h + 1], logit_ref[rows, 2 * h + 1 : 2 * h + 2]], axis=0
    )
    return 1.0 / (1.0 + jnp.exp(-x)), 1.0 / (1.0 + jnp.exp(x))


def crows(c):
    return pl.ds(pl.multiple_of(c * CR, CR), CR)


def trows(c):
    return pl.ds(pl.multiple_of(c * CT, CT), CT)


def place():
    s = lax.axis_index("seq")
    core = lax.rem(s, 2)
    y = lax.rem(lax.div(s, 2), 4)
    x = lax.div(s, 8)
    return x, y, core


def at(x, y, core):
    return (x * 4 + y) * 2 + core


def meet(x, y, core, z):
    barrier = pltpu.get_barrier_semaphore()
    peers = [{"seq": at(x, y, 1 - core)}]
    for d in (1, 2, 3):
        peers.append({"seq": at(x, lax.rem(y + d, 4), core)})
        peers.append({"seq": at(lax.rem(x + d, 4), y, core)})
    peers.append({"head": lax.rem(z + 1, 8)})
    peers.append({"head": lax.rem(z + 7, 8)})
    for p in peers:
        pl.semaphore_signal(barrier, inc=1, device_id=p, device_id_type=MESH)
    pl.semaphore_wait(barrier, len(peers))


RIGHT, LEFT = 0, 1
HALF = 256


def beside(z, way):
    return {"head": lax.rem(z + (1 if way == RIGHT else 7), 8)}


def gather_unit(buf, sems, z, way, d, j):
    src, dst = (d - 1, d) if way == RIGHT else ((9 - d) % 8, 8 - d)
    rows = pl.ds(j * HALF, HALF)
    return pltpu.make_async_remote_copy(
        src_ref=buf.at[src, rows],
        dst_ref=buf.at[dst, rows],
        send_sem=sems.at[0, way, d - 1, j],
        recv_sem=sems.at[1, way, d - 1, j],
        device_id=beside(z, way),
        device_id_type=MESH,
    )


def gather_has(way, d, j):
    return d < 4 or (d == 4 and j == way)


def gather_start(buf, sems, z):
    for j in (0, 1):
        for way in (RIGHT, LEFT):
            gather_unit(buf, sems, z, way, 1, j).start()


def gather_step(buf, sems, z, d, halves=(0, 1)):
    for j in halves:
        for way in (RIGHT, LEFT):
            if gather_has(way, d, j):
                gather_unit(buf, sems, z, way, d, j).wait_recv()
                if gather_has(way, d + 1, j):
                    gather_unit(buf, sems, z, way, d + 1, j).start()


def gather_end(buf, sems, z):
    for d in (1, 2, 3, 4):
        for j in (0, 1):
            for way in (RIGHT, LEFT):
                if gather_has(way, d, j):
                    gather_unit(buf, sems, z, way, d, j).wait_send()


class Scatter:
    def __init__(self, own, out, col, sent, came, sems, z):
        self.own, self.out, self.col, self.z = own, out, col, z
        self.sent, self.came, self.sems = sent, came, sems

    def unit(self, way, s, j):
        rows = pl.ds(j * HALF, HALF)
        return pltpu.make_async_remote_copy(
            src_ref=self.sent.at[way, s, rows],
            dst_ref=self.came.at[way, s, rows],
            send_sem=self.sems.at[0, way, s, j],
            recv_sem=self.sems.at[1, way, s, j],
            device_id=beside(self.z, way),
            device_id_type=MESH,
        )

    def has(self, way, s, j):
        return s > 0 or j == way

    def step(self, way, s, j):
        if not self.has(way, s, j):
            return
        rows = slice(j * HALF, (j + 1) * HALF)
        dest = lax.rem(self.z + ((4 - s) if way == RIGHT else (4 + s)), 8)
        term = self.own(dest, j)
        if s > 0 and self.has(way, s - 1, j):
            self.unit(way, s - 1, j).wait_recv()
            term = term + self.came[way, s - 1, rows].astype(F32)
        self.sent[way, s, rows] = term.astype(BF16)
        self.unit(way, s, j).start()

    def finish(self, j):
        rows = slice(j * HALF, (j + 1) * HALF)
        term = self.own(self.z, j)
        for way in (RIGHT, LEFT):
            self.unit(way, 3, j).wait_recv()
            term = term + self.came[way, 3, rows].astype(F32)
        self.out[rows, self.col : self.col + HALF] = term.astype(BF16)

    def end(self):
        for way in (RIGHT, LEFT):
            for s in range(4):
                for j in (0, 1):
                    if self.has(way, s, j):
                        self.unit(way, s, j).wait_send()


def send(src, dst, sems, i, seq):
    return pltpu.make_async_remote_copy(
        src_ref=src,
        dst_ref=dst,
        send_sem=sems.at[0, i],
        recv_sem=sems.at[1, i],
        device_id={"seq": seq},
        device_id_type=MESH,
    )


def compose(later, earlier, times=mm):
    r = times(later[:, :DK], earlier)
    return jnp.concatenate([r[:, :DK], r[:, DK:] + later[:, DK:].astype(F32)], axis=1)


def eye_nat():
    r = lax.broadcasted_iota(jnp.int32, (DK, DK), 0)
    c = lax.broadcasted_iota(jnp.int32, (DK, DK), 1)
    return jnp.where(r == c, 1.0, 0.0)


CONTRACT = (((1,), (1,)), ((), ()))


def layer_kernel(
    hid, pw, bw, gain, ow, cot,
    out,
    hids, cots, pw_v, ow_v, proj, logit, dn,
    q_i, k_i, w_i, uv_i, t_i, a_i, pm_i, po_i, mc_i, msave, qp_s, q2_s, o2_s,
    oc, mo, cslot, yslot_f, xslot_f, fin_f,
    s_s, u_s, do_s, y_s, e_s, d_s, esum, ec, yslot_b, xslot_b, fin_b,
    normed, gproj, glogit, msent, mcame, gsent, gcame,
    sems_h, sems_c, sems_f, sems_b, sems_m, sems_g, sems_w,
):
    heads = 2
    chunks = proj.shape[0] // CT
    x, y, core = place()
    z = lax.axis_index("head")
    pw_copy = pltpu.make_async_copy(pw, pw_v, sems_w.at[0])
    ow_copy = pltpu.make_async_copy(ow, ow_v, sems_w.at[1])
    pw_copy.start()
    ow_copy.start()
    hids[0] = hid[...]
    cots[0] = cot[...]
    meet(x, y, core, z)

    gather_start(hids, sems_h, z)
    pw_copy.wait()
    for d in range(5):
        if d > 0:
            gather_step(hids, sems_h, z, d)
        if d == 4:
            gather_start(cots, sems_c, z)
        for i in {d, (8 - d) % 8}:
            rows = pl.ds(pl.multiple_of(lax.rem(z + 8 - i, 8) * HALF, HALF), HALF)
            part = jnp.dot(hids[i], pw_v[rows, :], preferred_element_type=F32)
            part_b = lax.dot_general(hids[i], bw[:, rows], CONTRACT, preferred_element_type=F32)
            proj[...] = part if i == 0 else proj[...] + part
            logit[...] = part_b if i == 0 else logit[...] + part_b

    def chunk_batch(step, carry):
        @pl.when(step == 1)
        def _():
            gather_step(cots, sems_c, z, 1, (0,))

        r_at, c_at = orders(CR, CR, False, False)
        below = r_at > c_at
        diff = jnp.bitwise_xor(r_at, c_at)
        tr, tc = orders(CT, CR, True, False)
        visible = tc <= 2 * tr + 1
        eye = jnp.where(r_at == c_at, 1.0, 0.0)
        jobs = [(h, BATCH * step + cc) for cc in range(BATCH) for h in range(heads)]
        ks, bs, vs, qs = [], [], [], []
        for h, c in jobs:
            a, c1, c2, v1, v2 = head_rows(proj, c, h)
            q = a * unit_scale(a, 1e-6)
            k = jnp.concatenate([c1 * unit_scale(c1, 1e-6), c2 * unit_scale(c2, 1e-6)], axis=0)
            sig, _ = strengths(logit, c, h)
            ks.append(k)
            qs.append(q)
            bs.append(2.0 * sig)
            vs.append(jnp.concatenate([v1, v2], axis=0))
            q_i[h, trows(c), :] = q
            k_i[h, crows(c), :] = k
        kts = [k.T for k in ks]
        kt4 = [rhs(kt) for kt in kts]
        grams = [pmm(lhs(jnp.concatenate([k, q], axis=0)), b4) for k, q, b4 in zip(ks, qs, kt4)]
        for (h, c), g in zip(jobs, grams):
            a_i[h, trows(c), :] = jnp.where(visible, g[CR:], 0.0)
        ns = [jnp.where(below, b * g[:CR], 0.0) for b, g in zip(bs, grams)]
        ts = [eye - jnp.where(diff == 1, n, 0.0) for n in ns]
        level = 1
        while (1 << level) < CR:
            parts = [jnp.where((diff >> level) == 1, n, 0.0) for n in ns]
            inner = [mm(p, t) for p, t in zip(parts, ts)]
            outer = [mm(t, i) for t, i in zip(ts, inner)]
            ts = [t - o for t, o in zip(ts, outer)]
            level += 1
        wus = [mm(t, b * jnp.concatenate([k, v], axis=1)) for t, b, k, v in zip(ts, bs, ks, vs)]
        mos = [pmm(lhs(kt), rhs(wu)) for kt, wu in zip(kts, wus)]
        for (h, c), t, wu, m in zip(jobs, ts, wus, mos):
            t_i[h, crows(c), :] = t
            w_i[h, crows(c), :] = wu[:, :DK]
            uv_i[h, crows(c), :] = wu[:, DK:]
            mc_i[h, crows(c), :] = eye_nat() - m[:, :DK]
            oc[h, crows(c), :] = m[:, DK:]
        return carry

    lax.fori_loop(0, chunks // BATCH, chunk_batch, 0)

    gather_step(cots, sems_c, z, 1, (1,))

    for h in range(heads):
        mo[h, :, :DK] = eye_nat()
        mo[h, :, DK:] = jnp.zeros((DK, DK), F32)

    def prefix(c, carry):
        for h in range(heads):
            cur = mo[h]
            pm_i[h, crows(c), :] = cur[:, :DK]
            po_i[h, crows(c), :] = cur[:, DK:]
            r = mm(mc_i[h, crows(c), :], cur)
            mo[h, :, :DK] = r[:, :DK]
            mo[h, :, DK:] = r[:, DK:] + oc[h, crows(c), :]
        return carry

    lax.fori_loop(0, chunks, prefix, 0)

    c0 = send(mo.at[1 - core], cslot.at[core], sems_f, 0, at(x, y, 1 - core))
    c0.start()
    cslot[core] = mo[core]
    gather_step(cots, sems_c, z, 2, (0,))
    c0.wait()
    first = cslot[0]
    yslot_f[0] = compose(cslot[1], first).astype(BF16)
    sends = [
        send(yslot_f.at[0], yslot_f.at[d], sems_f, d, at(x, lax.rem(y + d, 4), core))
        for d in (1, 2, 3)
    ]
    for c in sends:
        c.start()

    gather_step(cots, sems_c, z, 2, (1,))

    def read_maps(step, carry):
        @pl.when(step == 1)
        def _():
            gather_step(cots, sems_c, z, 3, (0,))

        jobs = [(h, BATCH * step + cc) for cc in range(BATCH) for h in range(heads)]
        sees = [lhs(a_i[h, trows(c), :]) for h, c in jobs]
        aws = [pmm(a2, rhs(w_i[h, crows(c), :])) for (h, c), a2 in zip(jobs, sees)]
        aus = [pmm(a2, rhs(uv_i[h, crows(c), :])) for (h, c), a2 in zip(jobs, sees)]
        qps = [q_i[h, trows(c), :] - aw for (h, c), aw in zip(jobs, aws)]
        qp2 = [lhs(qp) for qp in qps]
        q2s = [pmm(a2, rhs(pm_i[h, crows(c), :])) for (h, c), a2 in zip(jobs, qp2)]
        o2s = [pmm(a2, rhs(po_i[h, crows(c), :])) for (h, c), a2 in zip(jobs, qp2)]
        for (h, c), qp, q2, o2, au in zip(jobs, qps, q2s, o2s, aus):
            qp_s[h, trows(c), :] = qp
            q2_s[h, trows(c), :] = q2
            o2_s[h, trows(c), :] = o2 + au
        return carry

    lax.fori_loop(0, chunks // BATCH, read_maps, 0)
    for c in sends:
        c.wait()
    gather_step(cots, sems_c, z, 3, (1,))
    got = [yslot_f[lax.rem(y + 4 - i, 4)] for i in range(4)]
    p1 = got[0].astype(F32)
    p2 = compose(got[1], p1, mmb)
    p3 = compose(got[2], p2, mmb)
    xslot_f[0] = compose(got[3], p3, mmb).astype(BF16)
    sends = [
        send(xslot_f.at[0], xslot_f.at[d], sems_f, 3 + d, at(lax.rem(x + d, 4), y, core))
        for d in (1, 2, 3)
    ]
    for c in sends:
        c.start()
    before = jnp.where(y == 1, p1, jnp.where(y == 2, p2, p3))
    m_y = [g[:, :DK].T for g in got]
    suf1 = mmb(m_y[2], m_y[3].astype(F32))
    suf0 = mmb(m_y[1], suf1)
    suf = jnp.where(y == 2, m_y[3].astype(F32), jnp.where(y == 1, suf1, suf0))
    for i in range(4):
        msave[i] = m_y[i]
    gather_step(cots, sems_c, z, 4)
    ow_copy.wait()
    for i in range(8):
        cols = pl.ds(pl.multiple_of(lax.rem(z + 8 - i, 8) * HALF, HALF), HALF)
        term = lax.dot_general(cots[i], ow_v[:, cols], CONTRACT, preferred_element_type=F32)
        dn[...] = term if i == 0 else dn[...] + term
    for c in sends:
        c.wait()
    gx = [xslot_f[lax.rem(x + 4 - i, 4)] for i in range(4)]
    s1 = gx[0][:, DK:].astype(F32)
    s2 = mmb(gx[1][:, :DK], s1) + gx[1][:, DK:].astype(F32)
    s3 = mmb(gx[2][:, :DK], s2) + gx[2][:, DK:].astype(F32)
    group = jnp.where(x == 0, 0.0, jnp.where(x == 1, s1, jnp.where(x == 2, s2, s3)))
    s_chip = jnp.where(y == 0, group, mm(before[:, :DK], group) + before[:, DK:])
    s_next = mm(first[:, :DK], s_chip) + first[:, DK:]
    fin_f[2] = jnp.where(core == 0, s_next, s_chip)
    c1 = send(fin_f.at[2], fin_f.at[core], sems_f, 7, at(x, y, 1 - core))
    c1.start()
    fin_f[core] = jnp.where(core == 0, s_chip, s_next)
    c1.wait()

    outs, scales = [], []
    for h in range(heads):
        o = mm(q2_s[h], fin_f[h]) + o2_s[h]
        r = lax.rsqrt(jnp.mean(o * o, axis=1, keepdims=True) + 1e-5)
        normed[:, h * DK : (h + 1) * DK] = (o * r * gain[h : h + 1, :]).astype(BF16)
        outs.append(o)
        scales.append(r)

    def mixed_term(dest, j):
        cols = pl.ds(pl.multiple_of(dest * HALF, HALF), HALF)
        return jnp.dot(
            normed[j * HALF : (j + 1) * HALF, :], ow_v[:, cols], preferred_element_type=F32
        )

    mixed = Scatter(mixed_term, out, 0, msent, mcame, sems_m, z)
    mixed.step(RIGHT, 0, 0)
    mixed.step(LEFT, 0, 1)
    mixed.step(RIGHT, 1, 1)
    mixed.step(LEFT, 1, 0)
    for h in range(heads):
        o, r = outs[h], scales[h]
        dy = dn[:, h * DK : (h + 1) * DK] * gain[h : h + 1, :]
        back = jnp.mean(o * dy, axis=1, keepdims=True)
        do = r * (dy - o * (r * r * back))
        do_s[h] = do
        esum[h] = mmt(q2_s[h], do)

    c0 = send(esum.at[1 - core], ec.at[core], sems_b, 0, at(x, y, 1 - core))
    c0.start()
    ec[core] = esum[core]
    m_c = [cslot[i, :, :DK].T for i in range(2)]
    c0.wait()
    e1 = ec[1]
    yslot_b[0] = (mm(m_c[0], e1) + ec[0]).astype(BF16)
    sends = [
        send(yslot_b.at[0], yslot_b.at[d], sems_b, d, at(x, lax.rem(y + d, 4), core))
        for d in (1, 2, 3)
    ]
    for c in sends:
        c.start()

    def inner_parts(step, carry):
        @pl.when(step == 1)
        def _():
            mixed.step(RIGHT, 1, 0)
            mixed.step(LEFT, 1, 1)

        jobs = [(h, BATCH * step + cc) for cc in range(BATCH) for h in range(heads)]
        starts = [rhs(fin_f[h]) for h in range(heads)]
        states = [
            pmm(lhs(pm_i[h, crows(c), :]), starts[h]) + po_i[h, crows(c), :] for h, c in jobs
        ]
        us = [uv_i[h, crows(c), :] - mm(w_i[h, crows(c), :], s) for (h, c), s in zip(jobs, states)]
        dos = [do_s[h, trows(c), :] for h, c in jobs]
        sides = [
            mmt(jnp.concatenate([a_i[h, trows(c), :], qp_s[h, trows(c), :]], axis=1), do)
            for (h, c), do in zip(jobs, dos)
        ]
        for (h, c), s, u, side in zip(jobs, states, us, sides):
            s_s[h, crows(c), :] = s
            u_s[h, crows(c), :] = u
            y_s[h, crows(c), :] = side[:CR]
            e_s[h, crows(c), :] = side[CR:]
        return carry

    lax.fori_loop(0, chunks // BATCH, inner_parts, 0)
    mixed.step(RIGHT, 2, 1)
    mixed.step(LEFT, 2, 0)
    for c in sends:
        c.wait()
    got = [yslot_b[lax.rem(y + 4 - i, 4)] for i in range(4)]
    r3 = got[3].astype(F32)
    r2 = mmb(msave[2], r3) + got[2].astype(F32)
    r1 = mmb(msave[1], r2) + got[1].astype(F32)
    xslot_b[0] = (mmb(msave[0], r1) + got[0].astype(F32)).astype(BF16)
    sends = [
        send(xslot_b.at[0], xslot_b.at[d], sems_b, 3 + d, at(lax.rem(x + d, 4), y, core))
        for d in (1, 2, 3)
    ]
    for c in sends:
        c.start()
    inside = jnp.where(y == 2, r3, jnp.where(y == 1, r2, r1))
    m_x = [xslot_f[lax.rem(x + 4 - i, 4), :, :DK].T for i in (1, 2)]
    mixed.step(RIGHT, 2, 0)
    mixed.step(LEFT, 2, 1)
    for c in sends:
        c.wait()
    gx = [xslot_b[lax.rem(x + 4 - i, 4)].astype(F32) for i in range(4)]
    x2 = gx[3]
    x1 = mmb(m_x[1], x2) + gx[2]
    x0 = mmb(m_x[0], x1) + gx[1]
    group = jnp.where(x == 3, 0.0, jnp.where(x == 2, x2, jnp.where(x == 1, x1, x0)))
    d_chip = jnp.where(y == 3, group, mm(suf, group) + inside)
    d_prev = mm(m_c[1], d_chip) + e1
    fin_b[2] = jnp.where(core == 1, d_prev, d_chip)
    c1 = send(fin_b.at[2], fin_b.at[core], sems_b, 7, at(x, y, 1 - core))
    c1.start()
    fin_b[core] = jnp.where(core == 1, d_chip, d_prev)
    mixed.step(RIGHT, 3, 1)
    mixed.step(LEFT, 3, 0)
    c1.wait()

    def chain(step, carry):
        c = chunks - 1 - step
        for h in range(heads):
            cur = fin_b[h]
            d_s[h, crows(c), :] = cur
            fin_b[h] = mmt(mc_i[h, crows(c), :], cur) + e_s[h, crows(c), :]
        return carry

    lax.fori_loop(0, chunks, chain, 0)

    def grad_term(dest, j):
        rows = slice(j * HALF, (j + 1) * HALF)
        part = pl.ds(pl.multiple_of(dest * HALF, HALF), HALF)
        return lax.dot_general(
            gproj[rows, :], pw_v[part, :], CONTRACT, preferred_element_type=F32
        ) + jnp.dot(glogit[rows, :], bw[:, part], preferred_element_type=F32)

    grads = Scatter(grad_term, out, HALF, gsent, gcame, sems_g, z)

    def backward(step, carry):
        @pl.when(step == 1)
        def _():
            mixed.step(RIGHT, 3, 0)
            mixed.step(LEFT, 3, 1)
            grads.step(RIGHT, 0, 0)
            grads.step(LEFT, 1, 0)

        r_at, c_at = orders(CR, CR, False, False)
        below = r_at > c_at
        tr, tc = orders(CT, CR, True, False)
        visible = tc <= 2 * tr + 1
        jobs = [(h, BATCH * step + cc) for cc in range(BATCH) for h in range(heads)]
        ks = [k_i[h, crows(c), :] for h, c in jobs]
        k4 = [rhs(k) for k in ks]
        ds = [d_s[h, crows(c), :] for h, c in jobs]
        us = [u_s[h, crows(c), :] for h, c in jobs]
        dus = [mm(k, d) + y_s[h, crows(c), :] for (h, c), k, d in zip(jobs, ks, ds)]
        zs = [mmt(t_i[h, crows(c), :], du) for (h, c), du in zip(jobs, dus)]
        sigs = [strengths(logit, c, h) for h, c in jobs]
        bzs = [2.0 * sg[0] * z for sg, z in zip(sigs, zs)]
        dos = [do_s[h, trows(c), :] for h, c in jobs]
        both = [lhs(jnp.concatenate([bz, do], axis=0)) for bz, do in zip(bzs, dos)]
        pus = [pmm(b2, rhs(u.T)) for b2, u in zip(both, us)]
        pss = [pmm(b2, rhs(s_s[h, crows(c), :].T)) for (h, c), b2 in zip(jobs, both)]
        pbs = [jnp.where(below, p[:CR], 0.0) for p in pus]
        das = [jnp.where(visible, p[CR:], 0.0) for p in pus]
        mixes = [
            pmm(lhs(jnp.concatenate([pb + pb.T, da], axis=0)), kk)
            for pb, da, kk in zip(pbs, das, k4)
        ]
        dks = [
            mm(u, d.T) - ps[:CR] - mx[:CR] + mmt(da, q_i[h, trows(c), :])
            for (h, c), u, d, ps, mx, da in zip(jobs, us, ds, pss, mixes, das)
        ]
        dqs = [mx[CR:] + ps[CR:] for mx, ps in zip(mixes, pss)]
        for (h, c), k, u, z, bz, sg, dk, dq in zip(jobs, ks, us, zs, bzs, sigs, dks, dqs):
            a, c1, c2, _, _ = head_rows(proj, c, h)
            q = q_i[h, trows(c), :]
            sa = unit_scale(a, 1e-6)
            sc = jnp.concatenate([unit_scale(c1, 1e-6), unit_scale(c2, 1e-6)], axis=0)
            ga = sa * (dq - q * jnp.sum(q * dq, axis=1, keepdims=True))
            gc = sc * (dk - k * jnp.sum(k * dk, axis=1, keepdims=True))
            base = h * 5 * DK
            gproj[trows(c), base : base + DK] = ga.astype(BF16)
            gproj[trows(c), base + DK : base + 2 * DK] = gc[:CT].astype(BF16)
            gproj[trows(c), base + 2 * DK : base + 3 * DK] = gc[CT:].astype(BF16)
            gproj[trows(c), base + 3 * DK : base + 4 * DK] = bz[:CT].astype(BF16)
            gproj[trows(c), base + 4 * DK : base + 5 * DK] = bz[CT:].astype(BF16)
            gl = jnp.sum(z * u, axis=1, keepdims=True) * sg[1]
            glogit[trows(c), 2 * h : 2 * h + 1] = gl[:CT].astype(BF16)
            glogit[trows(c), 2 * h + 1 : 2 * h + 2] = gl[CT:].astype(BF16)
        return carry

    lax.fori_loop(0, chunks // BATCH, backward, 0)
    grads.step(RIGHT, 1, 1)
    grads.step(LEFT, 0, 1)
    grads.step(RIGHT, 1, 0)
    grads.step(LEFT, 2, 0)
    mixed.finish(0)
    mixed.finish(1)
    grads.step(RIGHT, 2, 0)
    grads.step(LEFT, 3, 0)
    grads.step(RIGHT, 2, 1)
    grads.step(LEFT, 1, 1)
    grads.step(RIGHT, 3, 0)
    grads.step(LEFT, 2, 1)
    grads.step(RIGHT, 3, 1)
    grads.step(LEFT, 3, 1)
    grads.finish(0)
    grads.finish(1)
    mixed.end()
    grads.end()
    gather_end(hids, sems_h, z)
    gather_end(cots, sems_c, z)


def params(collective_id, mib):
    return pltpu.CompilerParams(
        collective_id=collective_id, has_side_effects=True, vmem_limit_bytes=mib << 20
    )


def local(hidden_in, proj_weight, beta_weight, norm_gain, out_weight, cotangent):
    rows = hidden_in.shape[0]
    buf = lambda *shape: pltpu.VMEM(shape, F32)
    low = lambda *shape: pltpu.VMEM(shape, BF16)
    dma = lambda *shape: pltpu.SemaphoreType.DMA(shape)
    part, full = buf(2, rows, DK), buf(2, REFL * rows, DK)
    square, wide = buf(2, DK, DK), buf(2, DK, 2 * DK)
    anywhere = pl.BlockSpec(memory_space=pl.ANY)
    both = pl.pallas_call(
        layer_kernel,
        out_shape=jax.ShapeDtypeStruct((rows, 2 * HALF), BF16),
        in_specs=[VM, anywhere, VM, VM, anywhere, VM],
        out_specs=VM,
        scratch_shapes=[
            low(8, rows, HALF), low(8, rows, HALF), low(*proj_weight.shape), low(*out_weight.shape),
            buf(rows, proj_weight.shape[1]), buf(rows, 4), buf(rows, 2 * DK),
            part, full, full, full, full, part, full, full, full, low(4, DK, DK), part, part, part,
            full, wide, wide, low(4, DK, 2 * DK), low(4, DK, 2 * DK), buf(3, DK, DK),
            full, full, part, full, full, full, square, square, low(4, DK, DK), low(4, DK, DK), buf(3, DK, DK),
            low(rows, 2 * DK), low(rows, 10 * DK), low(rows, 4),
            low(2, 4, rows, HALF), low(2, 4, rows, HALF),
            low(2, 4, rows, HALF), low(2, 4, rows, HALF),
            dma(2, 2, 4, 2), dma(2, 2, 4, 2), dma(2, 8), dma(2, 8),
            dma(2, 2, 4, 2), dma(2, 2, 4, 2), dma(2),
        ],
        compiler_params=params(1, 60),
    )(hidden_in, proj_weight, beta_weight.T, norm_gain.reshape(2, DK), out_weight, cotangent)
    return both[:, :HALF], both[:, HALF:]


def solution(mesh):
    placed = (
        P("seq", "head"),
        P(None, "head"),
        P(None, "head"),
        P("head"),
        P("head", None),
        P("seq", "head"),
    )
    return jax.shard_map(
        local,
        mesh=mesh,
        in_specs=placed,
        out_specs=(P("seq", "head"), P("seq", "head")),
        check_vma=False,
    )
```

```python
import jax
import jax.numpy as jnp
from jax import lax
from jax.experimental import pallas as pl
from jax.experimental.pallas import tpu as pltpu
from jax.sharding import PartitionSpec as P

DK = 128
REFL = 2
CT = 64
CR = CT * REFL
PASS = 8
BATCH = 4
MESH = pl.DeviceIdType.MESH
F32 = jnp.float32
BF16 = jnp.bfloat16
VM = pl.BlockSpec(memory_space=pltpu.VMEM)


def split(a):
    hi = a.astype(BF16)
    lo = (a - hi.astype(F32)).astype(BF16)
    return hi, lo


def lhs(a):
    hi, lo = split(a)
    return jnp.concatenate([hi, lo], axis=1)


def rhs(b):
    hi, lo = split(b)
    row = jnp.concatenate([hi, lo], axis=1)
    return jnp.concatenate([row, row], axis=0)


def pmm(a2, b4):
    n = b4.shape[1] // 2
    r = jnp.dot(a2, b4, preferred_element_type=F32)
    return r[:, :n] + r[:, n:]


def mm(a, b):
    return pmm(lhs(a), rhs(b))


def mmt(a, b):
    return pmm(lhs(a.T), rhs(b))


def mmb(a, b):
    hi, lo = split(b)
    n = b.shape[1]
    r = jnp.dot(a, jnp.concatenate([hi, lo], axis=1), preferred_element_type=F32)
    return r[:, :n] + r[:, n:]


def orders(rows, cols, row_tokens, col_tokens):
    r = lax.broadcasted_iota(jnp.int32, (rows, cols), 0)
    c = lax.broadcasted_iota(jnp.int32, (rows, cols), 1)
    if row_tokens:
        r_at = r
    else:
        r_at = 2 * (r % CT) + r // CT
    c_at = 2 * (c % CT) + c // CT
    return r_at, c_at


def unit_scale(v, eps):
    return lax.rsqrt(jnp.sum(v * v, axis=1, keepdims=True) + eps)


def head_rows(proj_ref, c, h):
    rows = pl.ds(pl.multiple_of(c * CT, CT), CT)
    base = h * 5 * DK
    return [proj_ref[rows, base + i * DK : base + (i + 1) * DK] for i in range(5)]


def strengths(logit_ref, c, h):
    rows = pl.ds(pl.multiple_of(c * CT, CT), CT)
    x = jnp.concatenate(
        [logit_ref[rows, 2 * h : 2 * h + 1], logit_ref[rows, 2 * h + 1 : 2 * h + 2]], axis=0
    )
    return 1.0 / (1.0 + jnp.exp(-x)), 1.0 / (1.0 + jnp.exp(x))


def crows(c):
    return pl.ds(pl.multiple_of(c * CR, CR), CR)


def trows(c):
    return pl.ds(pl.multiple_of(c * CT, CT), CT)


def place():
    s = lax.axis_index("seq")
    core = lax.rem(s, 2)
    y = lax.rem(lax.div(s, 2), 4)
    x = lax.div(s, 8)
    return x, y, core


def at(x, y, core):
    return (x * 4 + y) * 2 + core


def meet(x, y, core, z):
    barrier = pltpu.get_barrier_semaphore()
    peers = [{"seq": at(x, y, 1 - core)}]
    for d in (1, 2, 3):
        peers.append({"seq": at(x, lax.rem(y + d, 4), core)})
        peers.append({"seq": at(lax.rem(x + d, 4), y, core)})
    peers.append({"head": lax.rem(z + 1, 8)})
    peers.append({"head": lax.rem(z + 7, 8)})
    for p in peers:
        pl.semaphore_signal(barrier, inc=1, device_id=p, device_id_type=MESH)
    pl.semaphore_wait(barrier, len(peers))


RIGHT, LEFT = 0, 1
HALF = 256


def beside(z, way):
    return {"head": lax.rem(z + (1 if way == RIGHT else 7), 8)}


def gather_unit(buf, sems, z, way, d, j):
    src, dst = (d - 1, d) if way == RIGHT else ((9 - d) % 8, 8 - d)
    rows = pl.ds(j * HALF, HALF)
    return pltpu.make_async_remote_copy(
        src_ref=buf.at[src, rows],
        dst_ref=buf.at[dst, rows],
        send_sem=sems.at[0, way, d - 1, j],
        recv_sem=sems.at[1, way, d - 1, j],
        device_id=beside(z, way),
        device_id_type=MESH,
    )


def gather_has(way, d, j):
    return d < 4 or (d == 4 and j == way)


def gather_start(buf, sems, z):
    for j in (0, 1):
        for way in (RIGHT, LEFT):
            gather_unit(buf, sems, z, way, 1, j).start()


def gather_step(buf, sems, z, d, halves=(0, 1)):
    for j in halves:
        for way in (RIGHT, LEFT):
            if gather_has(way, d, j):
                gather_unit(buf, sems, z, way, d, j).wait_recv()
                if gather_has(way, d + 1, j):
                    gather_unit(buf, sems, z, way, d + 1, j).start()


def gather_end(buf, sems, z):
    for d in (1, 2, 3, 4):
        for j in (0, 1):
            for way in (RIGHT, LEFT):
                if gather_has(way, d, j):
                    gather_unit(buf, sems, z, way, d, j).wait_send()


class Scatter:
    def __init__(self, own, out, col, sent, came, sems, z):
        self.own, self.out, self.col, self.z = own, out, col, z
        self.sent, self.came, self.sems = sent, came, sems

    def unit(self, way, s, j):
        rows = pl.ds(j * HALF, HALF)
        return pltpu.make_async_remote_copy(
            src_ref=self.sent.at[way, s, rows],
            dst_ref=self.came.at[way, s, rows],
            send_sem=self.sems.at[0, way, s, j],
            recv_sem=self.sems.at[1, way, s, j],
            device_id=beside(self.z, way),
            device_id_type=MESH,
        )

    def has(self, way, s, j):
        return s > 0 or j == way

    def step(self, way, s, j):
        if not self.has(way, s, j):
            return
        rows = slice(j * HALF, (j + 1) * HALF)
        dest = lax.rem(self.z + ((4 - s) if way == RIGHT else (4 + s)), 8)
        term = self.own(dest, j)
        if s > 0 and self.has(way, s - 1, j):
            self.unit(way, s - 1, j).wait_recv()
            term = term + self.came[way, s - 1, rows].astype(F32)
        self.sent[way, s, rows] = term.astype(BF16)
        self.unit(way, s, j).start()

    def finish(self, j):
        rows = slice(j * HALF, (j + 1) * HALF)
        term = self.own(self.z, j)
        for way in (RIGHT, LEFT):
            self.unit(way, 3, j).wait_recv()
            term = term + self.came[way, 3, rows].astype(F32)
        self.out[rows, self.col : self.col + HALF] = term.astype(BF16)

    def end(self):
        for way in (RIGHT, LEFT):
            for s in range(4):
                for j in (0, 1):
                    if self.has(way, s, j):
                        self.unit(way, s, j).wait_send()


def send(src, dst, sems, i, seq):
    return pltpu.make_async_remote_copy(
        src_ref=src,
        dst_ref=dst,
        send_sem=sems.at[0, i],
        recv_sem=sems.at[1, i],
        device_id={"seq": seq},
        device_id_type=MESH,
    )


def compose(later, earlier, times=mm):
    r = times(later[:, :DK], earlier)
    return jnp.concatenate([r[:, :DK], r[:, DK:] + later[:, DK:].astype(F32)], axis=1)


def eye_nat():
    r = lax.broadcasted_iota(jnp.int32, (DK, DK), 0)
    c = lax.broadcasted_iota(jnp.int32, (DK, DK), 1)
    return jnp.where(r == c, 1.0, 0.0)


CONTRACT = (((1,), (1,)), ((), ()))


def layer_kernel(
    hid, pw, bw, gain, ow, cot,
    out,
    hids, cots, pw_v, ow_v, proj, logit, dn,
    q_i, k_i, w_i, uv_i, t_i, a_i, pm_i, po_i, mc_i, msave, qp_s, q2_s, o2_s,
    oc, mo, cslot, yslot_f, xslot_f, fin_f,
    s_s, u_s, do_s, y_s, e_s, back_mo, esum, ec, yslot_b, xslot_b, fin_b,
    normed, gproj, glogit, msent, mcame, gsent, gcame,
    sems_h, sems_c, sems_f, sems_b, sems_m, sems_g, sems_w,
):
    heads = 2
    chunks = proj.shape[0] // CT
    x, y, core = place()
    z = lax.axis_index("head")
    pw_copy = pltpu.make_async_copy(pw, pw_v, sems_w.at[0])
    ow_copy = pltpu.make_async_copy(ow, ow_v, sems_w.at[1])
    pw_copy.start()
    ow_copy.start()
    hids[0] = hid[...]
    cots[0] = cot[...]
    meet(x, y, core, z)

    gather_start(hids, sems_h, z)
    pw_copy.wait()
    for d in range(5):
        if d > 0:
            gather_step(hids, sems_h, z, d)
        if d == 4:
            gather_start(cots, sems_c, z)
        for i in {d, (8 - d) % 8}:
            rows = pl.ds(pl.multiple_of(lax.rem(z + 8 - i, 8) * HALF, HALF), HALF)
            part = jnp.dot(hids[i], pw_v[rows, :], preferred_element_type=F32)
            part_b = lax.dot_general(hids[i], bw[:, rows], CONTRACT, preferred_element_type=F32)
            proj[...] = part if i == 0 else proj[...] + part
            logit[...] = part_b if i == 0 else logit[...] + part_b

    def chunk_batch(step, carry):
        r_at, c_at = orders(CR, CR, False, False)
        below = r_at > c_at
        diff = jnp.bitwise_xor(r_at, c_at)
        tr, tc = orders(CT, CR, True, False)
        visible = tc <= 2 * tr + 1
        eye = jnp.where(r_at == c_at, 1.0, 0.0)
        jobs = [(h, PASS * step + cc) for cc in range(PASS) for h in range(heads)]
        ks, bs, vs, qs = [], [], [], []
        for h, c in jobs:
            a, c1, c2, v1, v2 = head_rows(proj, c, h)
            q = a * unit_scale(a, 1e-6)
            k = jnp.concatenate([c1 * unit_scale(c1, 1e-6), c2 * unit_scale(c2, 1e-6)], axis=0)
            sig, _ = strengths(logit, c, h)
            ks.append(k)
            qs.append(q)
            bs.append(2.0 * sig)
            vs.append(jnp.concatenate([v1, v2], axis=0))
            q_i[h, trows(c), :] = q
            k_i[h, crows(c), :] = k
        kts = [k.T for k in ks]
        kt4 = [rhs(kt) for kt in kts]
        grams = [pmm(lhs(jnp.concatenate([k, q], axis=0)), b4) for k, q, b4 in zip(ks, qs, kt4)]
        for (h, c), g in zip(jobs, grams):
            a_i[h, trows(c), :] = jnp.where(visible, g[CR:], 0.0)
        ns = [jnp.where(below, b * g[:CR], 0.0) for b, g in zip(bs, grams)]
        ts = [eye - jnp.where(diff == 1, n, 0.0) for n in ns]
        level = 1
        while (1 << level) < CR:
            parts = [jnp.where((diff >> level) == 1, n, 0.0) for n in ns]
            inner = [mm(p, t) for p, t in zip(parts, ts)]
            outer = [mm(t, i) for t, i in zip(ts, inner)]
            ts = [t - o for t, o in zip(ts, outer)]
            level += 1
        wus = [mm(t, b * jnp.concatenate([k, v], axis=1)) for t, b, k, v in zip(ts, bs, ks, vs)]
        mos = [pmm(lhs(kt), rhs(wu)) for kt, wu in zip(kts, wus)]
        for (h, c), t, wu, m in zip(jobs, ts, wus, mos):
            t_i[h, crows(c), :] = t
            w_i[h, crows(c), :] = wu[:, :DK]
            uv_i[h, crows(c), :] = wu[:, DK:]
            mc_i[h, crows(c), :] = eye_nat() - m[:, :DK]
            oc[h, crows(c), :] = m[:, DK:]
        return carry

    lax.fori_loop(0, chunks // PASS, chunk_batch, 0)

    gather_step(cots, sems_c, z, 1)

    for h in range(heads):
        mo[h, :, :DK] = eye_nat()
        mo[h, :, DK:] = jnp.zeros((DK, DK), F32)

    def prefix(c, carry):
        for h in range(heads):
            cur = mo[h]
            pm_i[h, crows(c), :] = cur[:, :DK]
            po_i[h, crows(c), :] = cur[:, DK:]
            r = mm(mc_i[h, crows(c), :], cur)
            mo[h, :, :DK] = r[:, :DK]
            mo[h, :, DK:] = r[:, DK:] + oc[h, crows(c), :]
        return carry

    lax.fori_loop(0, chunks, prefix, 0)

    c0 = send(mo.at[1 - core], cslot.at[core], sems_f, 0, at(x, y, 1 - core))
    c0.start()
    cslot[core] = mo[core]
    gather_step(cots, sems_c, z, 2, (0,))
    c0.wait()
    first = cslot[0]
    yslot_f[0] = compose(cslot[1], first).astype(BF16)
    sends = [
        send(yslot_f.at[0], yslot_f.at[d], sems_f, d, at(x, lax.rem(y + d, 4), core))
        for d in (1, 2, 3)
    ]
    for c in sends:
        c.start()

    gather_step(cots, sems_c, z, 2, (1,))

    def read_maps(step, carry):
        jobs = [(h, PASS * step + cc) for cc in range(PASS) for h in range(heads)]
        sees = [lhs(a_i[h, trows(c), :]) for h, c in jobs]
        aws = [pmm(a2, rhs(w_i[h, crows(c), :])) for (h, c), a2 in zip(jobs, sees)]
        aus = [pmm(a2, rhs(uv_i[h, crows(c), :])) for (h, c), a2 in zip(jobs, sees)]
        qps = [q_i[h, trows(c), :] - aw for (h, c), aw in zip(jobs, aws)]
        qp2 = [lhs(qp) for qp in qps]
        q2s = [pmm(a2, rhs(pm_i[h, crows(c), :])) for (h, c), a2 in zip(jobs, qp2)]
        o2s = [pmm(a2, rhs(po_i[h, crows(c), :])) for (h, c), a2 in zip(jobs, qp2)]
        for (h, c), qp, q2, o2, au in zip(jobs, qps, q2s, o2s, aus):
            qp_s[h, trows(c), :] = qp
            q2_s[h, trows(c), :] = q2
            o2_s[h, trows(c), :] = o2 + au
        return carry

    lax.fori_loop(0, chunks // PASS, read_maps, 0)
    for c in sends:
        c.wait()
    gather_step(cots, sems_c, z, 3)
    got = [yslot_f[lax.rem(y + 4 - i, 4)] for i in range(4)]
    p1 = got[0].astype(F32)
    p2 = compose(got[1], p1, mmb)
    p3 = compose(got[2], p2, mmb)
    xslot_f[0] = compose(got[3], p3, mmb).astype(BF16)
    sends = [
        send(xslot_f.at[0], xslot_f.at[d], sems_f, 3 + d, at(lax.rem(x + d, 4), y, core))
        for d in (1, 2, 3)
    ]
    for c in sends:
        c.start()
    before = jnp.where(y == 1, p1, jnp.where(y == 2, p2, p3))
    m_y = [g[:, :DK].T for g in got]
    suf1 = mmb(m_y[2], m_y[3].astype(F32))
    suf0 = mmb(m_y[1], suf1)
    suf = jnp.where(y == 2, m_y[3].astype(F32), jnp.where(y == 1, suf1, suf0))
    for i in range(4):
        msave[i] = m_y[i]
    gather_step(cots, sems_c, z, 4)
    ow_copy.wait()
    for i in range(8):
        cols = pl.ds(pl.multiple_of(lax.rem(z + 8 - i, 8) * HALF, HALF), HALF)
        term = lax.dot_general(cots[i], ow_v[:, cols], CONTRACT, preferred_element_type=F32)
        dn[...] = term if i == 0 else dn[...] + term
    for c in sends:
        c.wait()
    gx = [xslot_f[lax.rem(x + 4 - i, 4)] for i in range(4)]
    s1 = gx[0][:, DK:].astype(F32)
    s2 = mmb(gx[1][:, :DK], s1) + gx[1][:, DK:].astype(F32)
    s3 = mmb(gx[2][:, :DK], s2) + gx[2][:, DK:].astype(F32)
    group = jnp.where(x == 0, 0.0, jnp.where(x == 1, s1, jnp.where(x == 2, s2, s3)))
    s_chip = jnp.where(y == 0, group, mm(before[:, :DK], group) + before[:, DK:])
    s_next = mm(first[:, :DK], s_chip) + first[:, DK:]
    fin_f[2] = jnp.where(core == 0, s_next, s_chip)
    c1 = send(fin_f.at[2], fin_f.at[core], sems_f, 7, at(x, y, 1 - core))
    c1.start()
    fin_f[core] = jnp.where(core == 0, s_chip, s_next)
    c1.wait()

    outs, scales = [], []
    for h in range(heads):
        o = mm(q2_s[h], fin_f[h]) + o2_s[h]
        r = lax.rsqrt(jnp.mean(o * o, axis=1, keepdims=True) + 1e-5)
        normed[:, h * DK : (h + 1) * DK] = (o * r * gain[h : h + 1, :]).astype(BF16)
        outs.append(o)
        scales.append(r)

    def mixed_term(dest, j):
        cols = pl.ds(pl.multiple_of(dest * HALF, HALF), HALF)
        return jnp.dot(
            normed[j * HALF : (j + 1) * HALF, :], ow_v[:, cols], preferred_element_type=F32
        )

    mixed = Scatter(mixed_term, out, 0, msent, mcame, sems_m, z)
    mixed.step(RIGHT, 0, 0)
    mixed.step(LEFT, 0, 1)
    mixed.step(RIGHT, 1, 1)
    mixed.step(LEFT, 1, 0)
    for h in range(heads):
        o, r = outs[h], scales[h]
        dy = dn[:, h * DK : (h + 1) * DK] * gain[h : h + 1, :]
        back = jnp.mean(o * dy, axis=1, keepdims=True)
        do = r * (dy - o * (r * r * back))
        do_s[h] = do
        esum[h] = mmt(q2_s[h], do)

    c0 = send(esum.at[1 - core], ec.at[core], sems_b, 0, at(x, y, 1 - core))
    c0.start()
    ec[core] = esum[core]
    m_c = [cslot[i, :, :DK].T for i in range(2)]
    c0.wait()
    e1 = ec[1]
    yslot_b[0] = (mm(m_c[0], e1) + ec[0]).astype(BF16)
    sends = [
        send(yslot_b.at[0], yslot_b.at[d], sems_b, d, at(x, lax.rem(y + d, 4), core))
        for d in (1, 2, 3)
    ]
    for c in sends:
        c.start()

    def inner_parts(step, carry):
        jobs = [(h, PASS * step + cc) for cc in range(PASS) for h in range(heads)]
        starts = [rhs(fin_f[h]) for h in range(heads)]
        states = [
            pmm(lhs(pm_i[h, crows(c), :]), starts[h]) + po_i[h, crows(c), :] for h, c in jobs
        ]
        us = [uv_i[h, crows(c), :] - mm(w_i[h, crows(c), :], s) for (h, c), s in zip(jobs, states)]
        dos = [do_s[h, trows(c), :] for h, c in jobs]
        sides = [
            mmt(jnp.concatenate([a_i[h, trows(c), :], qp_s[h, trows(c), :]], axis=1), do)
            for (h, c), do in zip(jobs, dos)
        ]
        for (h, c), s, u, side in zip(jobs, states, us, sides):
            s_s[h, crows(c), :] = s
            u_s[h, crows(c), :] = u
            y_s[h, crows(c), :] = side[:CR]
            e_s[h, crows(c), :] = side[CR:]
        return carry

    mixed.step(RIGHT, 1, 0)
    mixed.step(LEFT, 1, 1)
    lax.fori_loop(0, chunks // PASS, inner_parts, 0)
    mixed.step(RIGHT, 2, 1)
    mixed.step(LEFT, 2, 0)
    for c in sends:
        c.wait()
    got = [yslot_b[lax.rem(y + 4 - i, 4)] for i in range(4)]
    r3 = got[3].astype(F32)
    r2 = mmb(msave[2], r3) + got[2].astype(F32)
    r1 = mmb(msave[1], r2) + got[1].astype(F32)
    xslot_b[0] = (mmb(msave[0], r1) + got[0].astype(F32)).astype(BF16)
    sends = [
        send(xslot_b.at[0], xslot_b.at[d], sems_b, 3 + d, at(lax.rem(x + d, 4), y, core))
        for d in (1, 2, 3)
    ]
    for c in sends:
        c.start()
    inside = jnp.where(y == 2, r3, jnp.where(y == 1, r2, r1))
    for h in range(heads):
        back_mo[h, :, :DK] = eye_nat()
        back_mo[h, :, DK:] = jnp.zeros((DK, DK), F32)

    def suffix(step, carry):
        c = chunks - 1 - step
        for h in range(heads):
            cur = back_mo[h]
            pm_i[h, crows(c), :] = cur[:, :DK]
            po_i[h, crows(c), :] = cur[:, DK:]
            r = mmt(mc_i[h, crows(c), :], cur)
            back_mo[h, :, :DK] = r[:, :DK]
            back_mo[h, :, DK:] = r[:, DK:] + e_s[h, crows(c), :]
        return carry

    lax.fori_loop(0, chunks, suffix, 0)
    m_x = [xslot_f[lax.rem(x + 4 - i, 4), :, :DK].T for i in (1, 2)]
    mixed.step(RIGHT, 2, 0)
    mixed.step(LEFT, 2, 1)
    for c in sends:
        c.wait()
    gx = [xslot_b[lax.rem(x + 4 - i, 4)].astype(F32) for i in range(4)]
    x2 = gx[3]
    x1 = mmb(m_x[1], x2) + gx[2]
    x0 = mmb(m_x[0], x1) + gx[1]
    group = jnp.where(x == 3, 0.0, jnp.where(x == 2, x2, jnp.where(x == 1, x1, x0)))
    d_chip = jnp.where(y == 3, group, mm(suf, group) + inside)
    d_prev = mm(m_c[1], d_chip) + e1
    fin_b[2] = jnp.where(core == 1, d_prev, d_chip)
    c1 = send(fin_b.at[2], fin_b.at[core], sems_b, 7, at(x, y, 1 - core))
    c1.start()
    fin_b[core] = jnp.where(core == 1, d_chip, d_prev)
    mixed.step(RIGHT, 3, 1)
    mixed.step(LEFT, 3, 0)
    c1.wait()

    def grad_term(dest, j):
        rows = slice(j * HALF, (j + 1) * HALF)
        part = pl.ds(pl.multiple_of(dest * HALF, HALF), HALF)
        return lax.dot_general(
            gproj[rows, :], pw_v[part, :], CONTRACT, preferred_element_type=F32
        ) + jnp.dot(glogit[rows, :], bw[:, part], preferred_element_type=F32)

    grads = Scatter(grad_term, out, HALF, gsent, gcame, sems_g, z)

    def backward(step, carry):
        @pl.when(step == 1)
        def _():
            mixed.step(RIGHT, 3, 0)
            mixed.step(LEFT, 3, 1)
            grads.step(RIGHT, 0, 0)
            grads.step(LEFT, 1, 0)

        r_at, c_at = orders(CR, CR, False, False)
        below = r_at > c_at
        tr, tc = orders(CT, CR, True, False)
        visible = tc <= 2 * tr + 1
        jobs = [(h, BATCH * step + cc) for cc in range(BATCH) for h in range(heads)]
        ks = [k_i[h, crows(c), :] for h, c in jobs]
        k4 = [rhs(k) for k in ks]
        ends = [rhs(fin_b[h]) for h in range(heads)]
        ds = [pmm(lhs(pm_i[h, crows(c), :]), ends[h]) + po_i[h, crows(c), :] for h, c in jobs]
        us = [u_s[h, crows(c), :] for h, c in jobs]
        dus = [mm(k, d) + y_s[h, crows(c), :] for (h, c), k, d in zip(jobs, ks, ds)]
        zs = [mmt(t_i[h, crows(c), :], du) for (h, c), du in zip(jobs, dus)]
        sigs = [strengths(logit, c, h) for h, c in jobs]
        bzs = [2.0 * sg[0] * z for sg, z in zip(sigs, zs)]
        dos = [do_s[h, trows(c), :] for h, c in jobs]
        both = [lhs(jnp.concatenate([bz, do], axis=0)) for bz, do in zip(bzs, dos)]
        pus = [pmm(b2, rhs(u.T)) for b2, u in zip(both, us)]
        pss = [pmm(b2, rhs(s_s[h, crows(c), :].T)) for (h, c), b2 in zip(jobs, both)]
        pbs = [jnp.where(below, p[:CR], 0.0) for p in pus]
        das = [jnp.where(visible, p[CR:], 0.0) for p in pus]
        mixes = [
            pmm(lhs(jnp.concatenate([pb + pb.T, da], axis=0)), kk)
            for pb, da, kk in zip(pbs, das, k4)
        ]
        dks = [
            mm(u, d.T) - ps[:CR] - mx[:CR] + mmt(da, q_i[h, trows(c), :])
            for (h, c), u, d, ps, mx, da in zip(jobs, us, ds, pss, mixes, das)
        ]
        dqs = [mx[CR:] + ps[CR:] for mx, ps in zip(mixes, pss)]
        for (h, c), k, u, z, bz, sg, dk, dq in zip(jobs, ks, us, zs, bzs, sigs, dks, dqs):
            a, c1, c2, _, _ = head_rows(proj, c, h)
            q = q_i[h, trows(c), :]
            sa = unit_scale(a, 1e-6)
            sc = jnp.concatenate([unit_scale(c1, 1e-6), unit_scale(c2, 1e-6)], axis=0)
            ga = sa * (dq - q * jnp.sum(q * dq, axis=1, keepdims=True))
            gc = sc * (dk - k * jnp.sum(k * dk, axis=1, keepdims=True))
            base = h * 5 * DK
            gproj[trows(c), base : base + DK] = ga.astype(BF16)
            gproj[trows(c), base + DK : base + 2 * DK] = gc[:CT].astype(BF16)
            gproj[trows(c), base + 2 * DK : base + 3 * DK] = gc[CT:].astype(BF16)
            gproj[trows(c), base + 3 * DK : base + 4 * DK] = bz[:CT].astype(BF16)
            gproj[trows(c), base + 4 * DK : base + 5 * DK] = bz[CT:].astype(BF16)
            gl = jnp.sum(z * u, axis=1, keepdims=True) * sg[1]
            glogit[trows(c), 2 * h : 2 * h + 1] = gl[:CT].astype(BF16)
            glogit[trows(c), 2 * h + 1 : 2 * h + 2] = gl[CT:].astype(BF16)
        return carry

    lax.fori_loop(0, chunks // BATCH, backward, 0)
    grads.step(RIGHT, 1, 1)
    grads.step(LEFT, 0, 1)
    grads.step(RIGHT, 1, 0)
    grads.step(LEFT, 2, 0)
    mixed.finish(0)
    mixed.finish(1)
    grads.step(RIGHT, 2, 0)
    grads.step(LEFT, 3, 0)
    grads.step(RIGHT, 2, 1)
    grads.step(LEFT, 1, 1)
    grads.step(RIGHT, 3, 0)
    grads.step(LEFT, 2, 1)
    grads.step(RIGHT, 3, 1)
    grads.step(LEFT, 3, 1)
    grads.finish(0)
    grads.finish(1)
    mixed.end()
    grads.end()
    gather_end(hids, sems_h, z)
    gather_end(cots, sems_c, z)


def params(collective_id, mib):
    return pltpu.CompilerParams(
        collective_id=collective_id, has_side_effects=True, vmem_limit_bytes=mib << 20
    )


def local(hidden_in, proj_weight, beta_weight, norm_gain, out_weight, cotangent):
    rows = hidden_in.shape[0]
    buf = lambda *shape: pltpu.VMEM(shape, F32)
    low = lambda *shape: pltpu.VMEM(shape, BF16)
    dma = lambda *shape: pltpu.SemaphoreType.DMA(shape)
    part, full = buf(2, rows, DK), buf(2, REFL * rows, DK)
    square, wide = buf(2, DK, DK), buf(2, DK, 2 * DK)
    anywhere = pl.BlockSpec(memory_space=pl.ANY)
    both = pl.pallas_call(
        layer_kernel,
        out_shape=jax.ShapeDtypeStruct((rows, 2 * HALF), BF16),
        in_specs=[VM, anywhere, VM, VM, anywhere, VM],
        out_specs=VM,
        scratch_shapes=[
            low(8, rows, HALF), low(8, rows, HALF), low(*proj_weight.shape), low(*out_weight.shape),
            buf(rows, proj_weight.shape[1]), buf(rows, 4), buf(rows, 2 * DK),
            part, full, full, full, full, part, full, full, full, low(4, DK, DK), part, part, part,
            full, wide, wide, low(4, DK, 2 * DK), low(4, DK, 2 * DK), buf(3, DK, DK),
            full, full, part, full, full, wide, square, square, low(4, DK, DK), low(4, DK, DK), buf(3, DK, DK),
            low(rows, 2 * DK), low(rows, 10 * DK), low(rows, 4),
            low(2, 4, rows, HALF), low(2, 4, rows, HALF),
            low(2, 4, rows, HALF), low(2, 4, rows, HALF),
            dma(2, 2, 4, 2), dma(2, 2, 4, 2), dma(2, 8), dma(2, 8),
            dma(2, 2, 4, 2), dma(2, 2, 4, 2), dma(2),
        ],
        compiler_params=params(1, 60),
    )(hidden_in, proj_weight, beta_weight.T, norm_gain.reshape(2, DK), out_weight, cotangent)
    return both[:, :HALF], both[:, HALF:]


def solution(mesh):
    placed = (
        P("seq", "head"),
        P(None, "head"),
        P(None, "head"),
        P("head"),
        P("head", None),
        P("seq", "head"),
    )
    return jax.shard_map(
        local,
        mesh=mesh,
        in_specs=placed,
        out_specs=(P("seq", "head"), P("seq", "head")),
        check_vma=False,
    )
```

```python
import jax
import jax.numpy as jnp
from jax import lax
from jax.experimental import pallas as pl
from jax.experimental.pallas import tpu as pltpu
from jax.sharding import PartitionSpec as P

DK = 128
REFL = 2
CT = 64
CR = CT * REFL
PASS = 8
BATCH = 4
MESH = pl.DeviceIdType.MESH
F32 = jnp.float32
BF16 = jnp.bfloat16
VM = pl.BlockSpec(memory_space=pltpu.VMEM)


def split(a):
    hi = a.astype(BF16)
    lo = (a - hi.astype(F32)).astype(BF16)
    return hi, lo


def lhs(a):
    hi, lo = split(a)
    return jnp.concatenate([hi, lo], axis=1)


def rhs(b):
    hi, lo = split(b)
    row = jnp.concatenate([hi, lo], axis=1)
    return jnp.concatenate([row, row], axis=0)


def pmm(a2, b4):
    n = b4.shape[1] // 2
    r = jnp.dot(a2, b4, preferred_element_type=F32)
    return r[:, :n] + r[:, n:]


def mm(a, b):
    return pmm(lhs(a), rhs(b))


def mmt(a, b):
    return pmm(lhs(a.T), rhs(b))


def mmb(a, b):
    hi, lo = split(b)
    n = b.shape[1]
    r = jnp.dot(a, jnp.concatenate([hi, lo], axis=1), preferred_element_type=F32)
    return r[:, :n] + r[:, n:]


def orders(rows, cols, row_tokens, col_tokens):
    r = lax.broadcasted_iota(jnp.int32, (rows, cols), 0)
    c = lax.broadcasted_iota(jnp.int32, (rows, cols), 1)
    if row_tokens:
        r_at = r
    else:
        r_at = 2 * (r % CT) + r // CT
    c_at = 2 * (c % CT) + c // CT
    return r_at, c_at


def unit_scale(v, eps):
    return lax.rsqrt(jnp.sum(v * v, axis=1, keepdims=True) + eps)


def head_rows(proj_ref, c, h):
    rows = pl.ds(pl.multiple_of(c * CT, CT), CT)
    base = h * 5 * DK
    return [proj_ref[rows, base + i * DK : base + (i + 1) * DK] for i in range(5)]


def strengths(logit_ref, c, h):
    rows = pl.ds(pl.multiple_of(c * CT, CT), CT)
    x = jnp.concatenate(
        [logit_ref[rows, 2 * h : 2 * h + 1], logit_ref[rows, 2 * h + 1 : 2 * h + 2]], axis=0
    )
    return 1.0 / (1.0 + jnp.exp(-x)), 1.0 / (1.0 + jnp.exp(x))


def crows(c):
    return pl.ds(pl.multiple_of(c * CR, CR), CR)


def trows(c):
    return pl.ds(pl.multiple_of(c * CT, CT), CT)


def place():
    s = lax.axis_index("seq")
    core = lax.rem(s, 2)
    y = lax.rem(lax.div(s, 2), 4)
    x = lax.div(s, 8)
    return x, y, core


def at(x, y, core):
    return (x * 4 + y) * 2 + core


def meet(x, y, core, z):
    barrier = pltpu.get_barrier_semaphore()
    peers = [{"seq": at(x, y, 1 - core)}]
    for d in (1, 2, 3):
        peers.append({"seq": at(x, lax.rem(y + d, 4), core)})
        peers.append({"seq": at(lax.rem(x + d, 4), y, core)})
    peers.append({"head": lax.rem(z + 1, 8)})
    peers.append({"head": lax.rem(z + 7, 8)})
    for p in peers:
        pl.semaphore_signal(barrier, inc=1, device_id=p, device_id_type=MESH)
    pl.semaphore_wait(barrier, len(peers))


RIGHT, LEFT = 0, 1
HALF = 256
PIECE = 128


def beside(z, way):
    return {"head": lax.rem(z + (1 if way == RIGHT else 7), 8)}


def gather_unit(buf, sems, z, way, d, j):
    src, dst = (d - 1, d) if way == RIGHT else ((9 - d) % 8, 8 - d)
    rows = pl.ds(j * PIECE, PIECE)
    return pltpu.make_async_remote_copy(
        src_ref=buf.at[src, rows],
        dst_ref=buf.at[dst, rows],
        send_sem=sems.at[0, way, d - 1, j],
        recv_sem=sems.at[1, way, d - 1, j],
        device_id=beside(z, way),
        device_id_type=MESH,
    )


def gather_has(way, d, j):
    return d < 4 or (d == 4 and j // 2 == way)


def gather_start(buf, sems, z):
    for j in range(4):
        for way in (RIGHT, LEFT):
            gather_unit(buf, sems, z, way, 1, j).start()


def gather_step(buf, sems, z, d, halves=(0, 1)):
    for j in [2 * half + i for half in halves for i in (0, 1)]:
        for way in (RIGHT, LEFT):
            if gather_has(way, d, j):
                gather_unit(buf, sems, z, way, d, j).wait_recv()
                if gather_has(way, d + 1, j):
                    gather_unit(buf, sems, z, way, d + 1, j).start()


def gather_end(buf, sems, z):
    for d in (1, 2, 3, 4):
        for j in range(4):
            for way in (RIGHT, LEFT):
                if gather_has(way, d, j):
                    gather_unit(buf, sems, z, way, d, j).wait_send()


class Scatter:
    def __init__(self, own, out, col, sent, came, sems, z):
        self.own, self.out, self.col, self.z = own, out, col, z
        self.sent, self.came, self.sems = sent, came, sems

    def unit(self, way, s, j):
        rows = pl.ds(j * PIECE, PIECE)
        return pltpu.make_async_remote_copy(
            src_ref=self.sent.at[way, s, rows],
            dst_ref=self.came.at[way, s, rows],
            send_sem=self.sems.at[0, way, s, j],
            recv_sem=self.sems.at[1, way, s, j],
            device_id=beside(self.z, way),
            device_id_type=MESH,
        )

    def has(self, way, s, j):
        return s > 0 or j == way

    def step(self, way, s, j):
        if not self.has(way, s, j):
            return
        dest = lax.rem(self.z + ((4 - s) if way == RIGHT else (4 + s)), 8)
        terms = self.own(dest, j)
        for i in (0, 1):
            p = 2 * j + i
            rows = slice(p * PIECE, (p + 1) * PIECE)
            term = terms[i * PIECE : (i + 1) * PIECE]
            if s > 0 and self.has(way, s - 1, j):
                self.unit(way, s - 1, p).wait_recv()
                term = term + self.came[way, s - 1, rows].astype(F32)
            self.sent[way, s, rows] = term.astype(BF16)
            self.unit(way, s, p).start()

    def finish(self, j):
        terms = self.own(self.z, j)
        for i in (0, 1):
            p = 2 * j + i
            rows = slice(p * PIECE, (p + 1) * PIECE)
            term = terms[i * PIECE : (i + 1) * PIECE]
            for way in (RIGHT, LEFT):
                self.unit(way, 3, p).wait_recv()
                term = term + self.came[way, 3, rows].astype(F32)
            self.out[rows, self.col : self.col + HALF] = term.astype(BF16)

    def end(self):
        for way in (RIGHT, LEFT):
            for s in range(4):
                for p in range(4):
                    if self.has(way, s, p // 2):
                        self.unit(way, s, p).wait_send()


def send(src, dst, sems, i, seq):
    return pltpu.make_async_remote_copy(
        src_ref=src,
        dst_ref=dst,
        send_sem=sems.at[0, i],
        recv_sem=sems.at[1, i],
        device_id={"seq": seq},
        device_id_type=MESH,
    )


def compose(later, earlier, times=mm):
    r = times(later[:, :DK], earlier)
    return jnp.concatenate([r[:, :DK], r[:, DK:] + later[:, DK:].astype(F32)], axis=1)


def eye_nat():
    r = lax.broadcasted_iota(jnp.int32, (DK, DK), 0)
    c = lax.broadcasted_iota(jnp.int32, (DK, DK), 1)
    return jnp.where(r == c, 1.0, 0.0)


CONTRACT = (((1,), (1,)), ((), ()))


def layer_kernel(
    hid, pw, bw, gain, ow, cot,
    out,
    hids, cots, pw_v, ow_v, proj, logit, dn,
    q_i, k_i, w_i, uv_i, t_i, a_i, pm_i, po_i, mc_i, msave, qp_s, q2_s, o2_s,
    oc, mo, cslot, yslot_f, xslot_f, fin_f,
    s_s, u_s, do_s, y_s, e_s, back_mo, esum, ec, yslot_b, xslot_b, fin_b,
    normed, gproj, glogit, msent, mcame, gsent, gcame,
    sems_h, sems_c, sems_f, sems_b, sems_m, sems_g, sems_w,
):
    heads = 2
    chunks = proj.shape[0] // CT
    x, y, core = place()
    z = lax.axis_index("head")
    pw_copy = pltpu.make_async_copy(pw, pw_v, sems_w.at[0])
    ow_copy = pltpu.make_async_copy(ow, ow_v, sems_w.at[1])
    pw_copy.start()
    ow_copy.start()
    hids[0] = hid[...]
    cots[0] = cot[...]
    meet(x, y, core, z)

    gather_start(hids, sems_h, z)
    pw_copy.wait()
    for d in range(5):
        if d > 0:
            gather_step(hids, sems_h, z, d)
        if d == 4:
            gather_start(cots, sems_c, z)
        for i in {d, (8 - d) % 8}:
            rows = pl.ds(pl.multiple_of(lax.rem(z + 8 - i, 8) * HALF, HALF), HALF)
            part = jnp.dot(hids[i], pw_v[rows, :], preferred_element_type=F32)
            part_b = lax.dot_general(hids[i], bw[:, rows], CONTRACT, preferred_element_type=F32)
            proj[...] = part if i == 0 else proj[...] + part
            logit[...] = part_b if i == 0 else logit[...] + part_b

    def chunk_batch(step, carry):
        r_at, c_at = orders(CR, CR, False, False)
        below = r_at > c_at
        diff = jnp.bitwise_xor(r_at, c_at)
        tr, tc = orders(CT, CR, True, False)
        visible = tc <= 2 * tr + 1
        eye = jnp.where(r_at == c_at, 1.0, 0.0)
        jobs = [(h, PASS * step + cc) for cc in range(PASS) for h in range(heads)]
        ks, bs, vs, qs = [], [], [], []
        for h, c in jobs:
            a, c1, c2, v1, v2 = head_rows(proj, c, h)
            q = a * unit_scale(a, 1e-6)
            k = jnp.concatenate([c1 * unit_scale(c1, 1e-6), c2 * unit_scale(c2, 1e-6)], axis=0)
            sig, _ = strengths(logit, c, h)
            ks.append(k)
            qs.append(q)
            bs.append(2.0 * sig)
            vs.append(jnp.concatenate([v1, v2], axis=0))
            q_i[h, trows(c), :] = q
            k_i[h, crows(c), :] = k
        kts = [k.T for k in ks]
        kt4 = [rhs(kt) for kt in kts]
        grams = [pmm(lhs(jnp.concatenate([k, q], axis=0)), b4) for k, q, b4 in zip(ks, qs, kt4)]
        for (h, c), g in zip(jobs, grams):
            a_i[h, trows(c), :] = jnp.where(visible, g[CR:], 0.0)
        ns = [jnp.where(below, b * g[:CR], 0.0) for b, g in zip(bs, grams)]
        ts = [eye - jnp.where(diff == 1, n, 0.0) for n in ns]
        level = 1
        while (1 << level) < CR:
            parts = [jnp.where((diff >> level) == 1, n, 0.0) for n in ns]
            inner = [mm(p, t) for p, t in zip(parts, ts)]
            outer = [mm(t, i) for t, i in zip(ts, inner)]
            ts = [t - o for t, o in zip(ts, outer)]
            level += 1
        wus = [mm(t, b * jnp.concatenate([k, v], axis=1)) for t, b, k, v in zip(ts, bs, ks, vs)]
        mos = [pmm(lhs(kt), rhs(wu)) for kt, wu in zip(kts, wus)]
        for (h, c), t, wu, m in zip(jobs, ts, wus, mos):
            t_i[h, crows(c), :] = t
            w_i[h, crows(c), :] = wu[:, :DK]
            uv_i[h, crows(c), :] = wu[:, DK:]
            mc_i[h, crows(c), :] = eye_nat() - m[:, :DK]
            oc[h, crows(c), :] = m[:, DK:]
        return carry

    lax.fori_loop(0, chunks // PASS, chunk_batch, 0)

    gather_step(cots, sems_c, z, 1)

    for h in range(heads):
        mo[h, :, :DK] = eye_nat()
        mo[h, :, DK:] = jnp.zeros((DK, DK), F32)

    def prefix(c, carry):
        for h in range(heads):
            cur = mo[h]
            pm_i[h, crows(c), :] = cur[:, :DK]
            po_i[h, crows(c), :] = cur[:, DK:]
            r = mm(mc_i[h, crows(c), :], cur)
            mo[h, :, :DK] = r[:, :DK]
            mo[h, :, DK:] = r[:, DK:] + oc[h, crows(c), :]
        return carry

    lax.fori_loop(0, chunks, prefix, 0)

    c0 = send(mo.at[1 - core], cslot.at[core], sems_f, 0, at(x, y, 1 - core))
    c0.start()
    cslot[core] = mo[core]
    gather_step(cots, sems_c, z, 2, (0,))
    c0.wait()
    first = cslot[0]
    yslot_f[0] = compose(cslot[1], first).astype(BF16)
    sends = [
        send(yslot_f.at[0], yslot_f.at[d], sems_f, d, at(x, lax.rem(y + d, 4), core))
        for d in (1, 2, 3)
    ]
    for c in sends:
        c.start()

    gather_step(cots, sems_c, z, 2, (1,))

    def read_maps(step, carry):
        jobs = [(h, PASS * step + cc) for cc in range(PASS) for h in range(heads)]
        sees = [lhs(a_i[h, trows(c), :]) for h, c in jobs]
        aws = [pmm(a2, rhs(w_i[h, crows(c), :])) for (h, c), a2 in zip(jobs, sees)]
        aus = [pmm(a2, rhs(uv_i[h, crows(c), :])) for (h, c), a2 in zip(jobs, sees)]
        qps = [q_i[h, trows(c), :] - aw for (h, c), aw in zip(jobs, aws)]
        qp2 = [lhs(qp) for qp in qps]
        q2s = [pmm(a2, rhs(pm_i[h, crows(c), :])) for (h, c), a2 in zip(jobs, qp2)]
        o2s = [pmm(a2, rhs(po_i[h, crows(c), :])) for (h, c), a2 in zip(jobs, qp2)]
        for (h, c), qp, q2, o2, au in zip(jobs, qps, q2s, o2s, aus):
            qp_s[h, trows(c), :] = qp
            q2_s[h, trows(c), :] = q2
            o2_s[h, trows(c), :] = o2 + au
        return carry

    lax.fori_loop(0, chunks // PASS, read_maps, 0)
    for c in sends:
        c.wait()
    gather_step(cots, sems_c, z, 3)
    got = [yslot_f[lax.rem(y + 4 - i, 4)] for i in range(4)]
    p1 = got[0].astype(F32)
    p2 = compose(got[1], p1, mmb)
    upper = compose(got[3], got[2].astype(F32), mmb)
    xslot_f[0] = compose(upper, p2).astype(BF16)
    sends = [
        send(xslot_f.at[0], xslot_f.at[d], sems_f, 3 + d, at(lax.rem(x + d, 4), y, core))
        for d in (1, 2, 3)
    ]
    for c in sends:
        c.start()
    p3 = compose(got[2], p2, mmb)
    before = jnp.where(y == 1, p1, jnp.where(y == 2, p2, p3))
    m_y = [g[:, :DK].T for g in got]
    suf1 = mmb(m_y[2], m_y[3].astype(F32))
    suf0 = mmb(m_y[1], suf1)
    suf = jnp.where(y == 2, m_y[3].astype(F32), jnp.where(y == 1, suf1, suf0))
    for i in range(4):
        msave[i] = m_y[i]
    gather_step(cots, sems_c, z, 4)
    ow_copy.wait()
    for i in range(8):
        cols = pl.ds(pl.multiple_of(lax.rem(z + 8 - i, 8) * HALF, HALF), HALF)
        term = lax.dot_general(cots[i], ow_v[:, cols], CONTRACT, preferred_element_type=F32)
        dn[...] = term if i == 0 else dn[...] + term
    for c in sends:
        c.wait()
    gx = [xslot_f[lax.rem(x + 4 - i, 4)] for i in range(4)]
    s1 = gx[0][:, DK:].astype(F32)
    s2 = mmb(gx[1][:, :DK], s1) + gx[1][:, DK:].astype(F32)
    s3 = mmb(gx[2][:, :DK], s2) + gx[2][:, DK:].astype(F32)
    group = jnp.where(x == 0, 0.0, jnp.where(x == 1, s1, jnp.where(x == 2, s2, s3)))
    s_chip = jnp.where(y == 0, group, mm(before[:, :DK], group) + before[:, DK:])
    s_next = mm(first[:, :DK], s_chip) + first[:, DK:]
    fin_f[2] = jnp.where(core == 0, s_next, s_chip)
    c1 = send(fin_f.at[2], fin_f.at[core], sems_f, 7, at(x, y, 1 - core))
    c1.start()
    fin_f[core] = jnp.where(core == 0, s_chip, s_next)
    c1.wait()

    outs, scales = [], []
    for h in range(heads):
        o = mm(q2_s[h], fin_f[h]) + o2_s[h]
        r = lax.rsqrt(jnp.mean(o * o, axis=1, keepdims=True) + 1e-5)
        normed[:, h * DK : (h + 1) * DK] = (o * r * gain[h : h + 1, :]).astype(BF16)
        outs.append(o)
        scales.append(r)

    def mixed_term(dest, j):
        cols = pl.ds(pl.multiple_of(dest * HALF, HALF), HALF)
        return jnp.dot(
            normed[j * HALF : (j + 1) * HALF, :], ow_v[:, cols], preferred_element_type=F32
        )

    mixed = Scatter(mixed_term, out, 0, msent, mcame, sems_m, z)
    mixed.step(RIGHT, 0, 0)
    mixed.step(LEFT, 0, 1)
    mixed.step(RIGHT, 1, 1)
    mixed.step(LEFT, 1, 0)
    for h in range(heads):
        o, r = outs[h], scales[h]
        dy = dn[:, h * DK : (h + 1) * DK] * gain[h : h + 1, :]
        back = jnp.mean(o * dy, axis=1, keepdims=True)
        do = r * (dy - o * (r * r * back))
        do_s[h] = do
        esum[h] = mmt(q2_s[h], do)

    c0 = send(esum.at[1 - core], ec.at[core], sems_b, 0, at(x, y, 1 - core))
    c0.start()
    ec[core] = esum[core]
    m_c = [cslot[i, :, :DK].T for i in range(2)]
    c0.wait()
    e1 = ec[1]
    yslot_b[0] = (mm(m_c[0], e1) + ec[0]).astype(BF16)
    sends = [
        send(yslot_b.at[0], yslot_b.at[d], sems_b, d, at(x, lax.rem(y + d, 4), core))
        for d in (1, 2, 3)
    ]
    for c in sends:
        c.start()

    def inner_parts(step, carry):
        jobs = [(h, PASS * step + cc) for cc in range(PASS) for h in range(heads)]
        starts = [rhs(fin_f[h]) for h in range(heads)]
        states = [
            pmm(lhs(pm_i[h, crows(c), :]), starts[h]) + po_i[h, crows(c), :] for h, c in jobs
        ]
        us = [uv_i[h, crows(c), :] - mm(w_i[h, crows(c), :], s) for (h, c), s in zip(jobs, states)]
        dos = [do_s[h, trows(c), :] for h, c in jobs]
        sides = [
            mmt(jnp.concatenate([a_i[h, trows(c), :], qp_s[h, trows(c), :]], axis=1), do)
            for (h, c), do in zip(jobs, dos)
        ]
        for (h, c), s, u, side in zip(jobs, states, us, sides):
            s_s[h, crows(c), :] = s
            u_s[h, crows(c), :] = u
            y_s[h, crows(c), :] = side[:CR]
            e_s[h, crows(c), :] = side[CR:]
        return carry

    mixed.step(RIGHT, 1, 0)
    mixed.step(LEFT, 1, 1)
    lax.fori_loop(0, chunks // PASS, inner_parts, 0)
    mixed.step(RIGHT, 2, 1)
    mixed.step(LEFT, 2, 0)
    for c in sends:
        c.wait()
    got = [yslot_b[lax.rem(y + 4 - i, 4)] for i in range(4)]
    r3 = got[3].astype(F32)
    r2 = mmb(msave[2], r3) + got[2].astype(F32)
    r1 = mmb(msave[1], r2) + got[1].astype(F32)
    xslot_b[0] = (mmb(msave[0], r1) + got[0].astype(F32)).astype(BF16)
    sends = [
        send(xslot_b.at[0], xslot_b.at[d], sems_b, 3 + d, at(lax.rem(x + d, 4), y, core))
        for d in (1, 2, 3)
    ]
    for c in sends:
        c.start()
    inside = jnp.where(y == 2, r3, jnp.where(y == 1, r2, r1))
    for h in range(heads):
        back_mo[h, :, :DK] = eye_nat()
        back_mo[h, :, DK:] = jnp.zeros((DK, DK), F32)

    def suffix(step, carry):
        c = chunks - 1 - step
        for h in range(heads):
            cur = back_mo[h]
            pm_i[h, crows(c), :] = cur[:, :DK]
            po_i[h, crows(c), :] = cur[:, DK:]
            r = mmt(mc_i[h, crows(c), :], cur)
            back_mo[h, :, :DK] = r[:, :DK]
            back_mo[h, :, DK:] = r[:, DK:] + e_s[h, crows(c), :]
        return carry

    lax.fori_loop(0, chunks, suffix, 0)
    m_x = [xslot_f[lax.rem(x + 4 - i, 4), :, :DK].T for i in (1, 2)]
    mixed.step(RIGHT, 2, 0)
    mixed.step(LEFT, 2, 1)
    for c in sends:
        c.wait()
    gx = [xslot_b[lax.rem(x + 4 - i, 4)].astype(F32) for i in range(4)]
    x2 = gx[3]
    x1 = mmb(m_x[1], x2) + gx[2]
    x0 = mmb(m_x[0], x1) + gx[1]
    group = jnp.where(x == 3, 0.0, jnp.where(x == 2, x2, jnp.where(x == 1, x1, x0)))
    d_chip = jnp.where(y == 3, group, mm(suf, group) + inside)
    d_prev = mm(m_c[1], d_chip) + e1
    fin_b[2] = jnp.where(core == 1, d_prev, d_chip)
    c1 = send(fin_b.at[2], fin_b.at[core], sems_b, 7, at(x, y, 1 - core))
    c1.start()
    fin_b[core] = jnp.where(core == 1, d_chip, d_prev)
    mixed.step(RIGHT, 3, 1)
    mixed.step(LEFT, 3, 0)
    c1.wait()

    def grad_term(dest, j):
        rows = slice(j * HALF, (j + 1) * HALF)
        part = pl.ds(pl.multiple_of(dest * HALF, HALF), HALF)
        return lax.dot_general(
            gproj[rows, :], pw_v[part, :], CONTRACT, preferred_element_type=F32
        ) + jnp.dot(glogit[rows, :], bw[:, part], preferred_element_type=F32)

    grads = Scatter(grad_term, out, HALF, gsent, gcame, sems_g, z)

    def backward(step, carry):
        @pl.when(step == 1)
        def _():
            mixed.step(RIGHT, 3, 0)
            mixed.step(LEFT, 3, 1)
            grads.step(RIGHT, 0, 0)
            grads.step(LEFT, 1, 0)

        r_at, c_at = orders(CR, CR, False, False)
        below = r_at > c_at
        tr, tc = orders(CT, CR, True, False)
        visible = tc <= 2 * tr + 1
        jobs = [(h, BATCH * step + cc) for cc in range(BATCH) for h in range(heads)]
        ks = [k_i[h, crows(c), :] for h, c in jobs]
        k4 = [rhs(k) for k in ks]
        ends = [rhs(fin_b[h]) for h in range(heads)]
        ds = [pmm(lhs(pm_i[h, crows(c), :]), ends[h]) + po_i[h, crows(c), :] for h, c in jobs]
        us = [u_s[h, crows(c), :] for h, c in jobs]
        dus = [mm(k, d) + y_s[h, crows(c), :] for (h, c), k, d in zip(jobs, ks, ds)]
        zs = [mmt(t_i[h, crows(c), :], du) for (h, c), du in zip(jobs, dus)]
        sigs = [strengths(logit, c, h) for h, c in jobs]
        bzs = [2.0 * sg[0] * z for sg, z in zip(sigs, zs)]
        dos = [do_s[h, trows(c), :] for h, c in jobs]
        both = [lhs(jnp.concatenate([bz, do], axis=0)) for bz, do in zip(bzs, dos)]
        pus = [pmm(b2, rhs(u.T)) for b2, u in zip(both, us)]
        pss = [pmm(b2, rhs(s_s[h, crows(c), :].T)) for (h, c), b2 in zip(jobs, both)]
        pbs = [jnp.where(below, p[:CR], 0.0) for p in pus]
        das = [jnp.where(visible, p[CR:], 0.0) for p in pus]
        mixes = [
            pmm(lhs(jnp.concatenate([pb + pb.T, da], axis=0)), kk)
            for pb, da, kk in zip(pbs, das, k4)
        ]
        dks = [
            mm(u, d.T) - ps[:CR] - mx[:CR] + mmt(da, q_i[h, trows(c), :])
            for (h, c), u, d, ps, mx, da in zip(jobs, us, ds, pss, mixes, das)
        ]
        dqs = [mx[CR:] + ps[CR:] for mx, ps in zip(mixes, pss)]
        for (h, c), k, u, z, bz, sg, dk, dq in zip(jobs, ks, us, zs, bzs, sigs, dks, dqs):
            a, c1, c2, _, _ = head_rows(proj, c, h)
            q = q_i[h, trows(c), :]
            sa = unit_scale(a, 1e-6)
            sc = jnp.concatenate([unit_scale(c1, 1e-6), unit_scale(c2, 1e-6)], axis=0)
            ga = sa * (dq - q * jnp.sum(q * dq, axis=1, keepdims=True))
            gc = sc * (dk - k * jnp.sum(k * dk, axis=1, keepdims=True))
            base = h * 5 * DK
            gproj[trows(c), base : base + DK] = ga.astype(BF16)
            gproj[trows(c), base + DK : base + 2 * DK] = gc[:CT].astype(BF16)
            gproj[trows(c), base + 2 * DK : base + 3 * DK] = gc[CT:].astype(BF16)
            gproj[trows(c), base + 3 * DK : base + 4 * DK] = bz[:CT].astype(BF16)
            gproj[trows(c), base + 4 * DK : base + 5 * DK] = bz[CT:].astype(BF16)
            gl = jnp.sum(z * u, axis=1, keepdims=True) * sg[1]
            glogit[trows(c), 2 * h : 2 * h + 1] = gl[:CT].astype(BF16)
            glogit[trows(c), 2 * h + 1 : 2 * h + 2] = gl[CT:].astype(BF16)
        return carry

    lax.fori_loop(0, chunks // BATCH, backward, 0)
    grads.step(RIGHT, 1, 1)
    grads.step(LEFT, 0, 1)
    grads.step(RIGHT, 1, 0)
    grads.step(LEFT, 2, 0)
    mixed.finish(0)
    mixed.finish(1)
    grads.step(RIGHT, 2, 0)
    grads.step(LEFT, 3, 0)
    grads.step(RIGHT, 2, 1)
    grads.step(LEFT, 1, 1)
    grads.step(RIGHT, 3, 0)
    grads.step(LEFT, 2, 1)
    grads.step(RIGHT, 3, 1)
    grads.step(LEFT, 3, 1)
    grads.finish(0)
    grads.finish(1)
    mixed.end()
    grads.end()
    gather_end(hids, sems_h, z)
    gather_end(cots, sems_c, z)


def params(collective_id, mib):
    return pltpu.CompilerParams(
        collective_id=collective_id, has_side_effects=True, vmem_limit_bytes=mib << 20
    )


def local(hidden_in, proj_weight, beta_weight, norm_gain, out_weight, cotangent):
    rows = hidden_in.shape[0]
    buf = lambda *shape: pltpu.VMEM(shape, F32)
    low = lambda *shape: pltpu.VMEM(shape, BF16)
    dma = lambda *shape: pltpu.SemaphoreType.DMA(shape)
    part, full = buf(2, rows, DK), buf(2, REFL * rows, DK)
    square, wide = buf(2, DK, DK), buf(2, DK, 2 * DK)
    anywhere = pl.BlockSpec(memory_space=pl.ANY)
    both = pl.pallas_call(
        layer_kernel,
        out_shape=jax.ShapeDtypeStruct((rows, 2 * HALF), BF16),
        in_specs=[VM, anywhere, VM, VM, anywhere, VM],
        out_specs=VM,
        scratch_shapes=[
            low(8, rows, HALF), low(8, rows, HALF), low(*proj_weight.shape), low(*out_weight.shape),
            buf(rows, proj_weight.shape[1]), buf(rows, 4), buf(rows, 2 * DK),
            part, full, full, full, full, part, full, full, full, low(4, DK, DK), part, part, part,
            full, wide, wide, low(4, DK, 2 * DK), low(4, DK, 2 * DK), buf(3, DK, DK),
            full, full, part, full, full, wide, square, square, low(4, DK, DK), low(4, DK, DK), buf(3, DK, DK),
            low(rows, 2 * DK), low(rows, 10 * DK), low(rows, 4),
            low(2, 4, rows, HALF), low(2, 4, rows, HALF),
            low(2, 4, rows, HALF), low(2, 4, rows, HALF),
            dma(2, 2, 4, 4), dma(2, 2, 4, 4), dma(2, 8), dma(2, 8),
            dma(2, 2, 4, 4), dma(2, 2, 4, 4), dma(2),
        ],
        compiler_params=params(1, 60),
    )(hidden_in, proj_weight, beta_weight.T, norm_gain.reshape(2, DK), out_weight, cotangent)
    return both[:, :HALF], both[:, HALF:]


def solution(mesh):
    placed = (
        P("seq", "head"),
        P(None, "head"),
        P(None, "head"),
        P("head"),
        P("head", None),
        P("seq", "head"),
    )
    return jax.shard_map(
        local,
        mesh=mesh,
        in_specs=placed,
        out_specs=(P("seq", "head"), P("seq", "head")),
        check_vma=False,
    )
```
